512 devices in a mesh: grp: 8 (over z_hi, x), gx: 8 (over z_lo, core), gy: 8 (over y).
Axes of the slice: x: 4, y: 8, z: 8 (z_hi: 2, z_lo: 4; z = z_hi * 4 + z_lo), core: 2. Of those that a mesh axis runs over, the one named last changes fastest.
Arguments:
- efield: float32 [8, 3, 128, 128, 128], P('grp', None, 'gx', 'gy'), may hold values from -6 to 6
- hfield: float32 [8, 3, 128, 128, 128], P('grp', None, 'gx', 'gy'), may hold values from -6 to 6
- fwd_dft: bfloat16 [8, 2, 2, 3, 128, 128, 128], P('grp', None, None, None, 'gx', 'gy'), may hold values from -6 to 6
- adj_dft: bfloat16 [8, 2, 2, 3, 128, 128, 128], P('grp', None, None, None, 'gx', 'gy'), may hold values from -6 to 6
- permittivity: float32 [128, 128, 128], P('gx', 'gy'), may hold values from 1 to 4
- source_amp: float32 [8, 128, 128], P('grp', 'gx', 'gy'), may hold values from -6 to 6
- source_plane: int32 [8], P('grp'), may hold values from 4 to 123
- freqs: float32 [8, 2], P('grp'), may hold values from 0.2 to 1.5
- pml_width: int32 [2], replicated, may hold values from 2 to 7
- design_blocks: int32 [128], replicated, may hold values from 0 to 255, as said below
Outputs:
- grad_step: float32 [2, 128, 128, 128], P(None, 'gx', 'gy')
The draws below stay inside these ranges and needn't reach their ends.
Inputs may be any that keep to these rules, and one draw needn't show every extreme that they name: `design_blocks`: distinct block numbers.
All inputs are finite; a program needn't handle non-finite values.
Results may differ from the reference program's by a relative error of at most 0.0003.
Values sent between devices are 32-bit elements; how exact they have to be, the bound alone decides.
A program may use at most 64 MiB of HBM per device.

```python
import math
import jax
import jax.numpy as jnp
from jax import lax

NZ = 128
BS = 8
STEPS = 2
GROUPS = 8
NX = 128
NY = 128
NB = 128


def draw_design_blocks(key, part):
    return jax.random.permutation(key, NX // BS * (NY // BS))[:NB].astype(jnp.int32)


def touch_ends(result, own_key, smallest, largest):
    index_at = [jax.random.randint(jax.random.fold_in(own_key, axis), (), 0, length) for axis, length in enumerate(result.shape)]
    widest = result.shape.index(max(result.shape))
    beside = index_at[:widest] + [(index_at[widest] + 1) % result.shape[widest]] + index_at[widest + 1:]
    return result.at[tuple(index_at)].set(smallest).at[tuple(beside)].set(largest)


def levels(rng, extent, split, least, largest):
    gain, own = 1.0, jax.random.fold_in(rng, 6)
    for position, shards_of in split:
        steps = jnp.exp(jax.random.uniform(jax.random.fold_in(own, position), (shards_of,), jnp.float32, least / len(split), largest / len(split)))
        gain = gain * jnp.repeat(steps, extent[position] // shards_of).reshape([-1 if axis == position else 1 for axis in range(len(extent))])
    return gain


def noise(own_key, shape, scale, most, cuts=(), kind=jnp.bfloat16):
    entries = jax.random.normal(own_key, shape, jnp.float32) * scale
    if len(cuts) > 0:
        entries = levels(own_key, shape, cuts, -0.22, 0.18) * entries
    return jnp.clip(entries, min=-most, max=most).astype(kind)


def setup_inputs(seed: int = 0) -> dict:
    arg_keys = jax.random.split(jax.random.key(seed), 11)
    efield = noise(arg_keys[0], (GROUPS, 3, NX, NY, NZ), 1.0, 6.0, ((0, 8), (2, 8), (3, 8)), jnp.float32)
    hfield = noise(arg_keys[1], (GROUPS, 3, NX, NY, NZ), 1.0, 6.0, ((0, 8), (2, 8), (3, 8)), jnp.float32)
    fwd_dft = noise(arg_keys[2], (GROUPS, 2, 2, 3, NX, NY, NZ), 1.0, 6.0, ((0, 8), (4, 8), (5, 8)))
    adj_dft = noise(arg_keys[3], (GROUPS, 2, 2, 3, NX, NY, NZ), 1.0, 6.0, ((0, 8), (4, 8), (5, 8)))
    permittivity = jnp.clip(1.0 + 3.0 * jax.random.uniform(arg_keys[4], (NX, NY, NZ), jnp.float32) ** levels(arg_keys[4], (NX, NY, NZ), ((0, 8), (1, 8)), -0.2, 0.2), 1.0, 4.0)
    source_amp = noise(arg_keys[5], (GROUPS, NX, NY), 1.0, 6.0, ((0, 8), (1, 8), (2, 8)), jnp.float32)
    source_plane = touch_ends(jax.random.randint(arg_keys[6], (GROUPS,), 4, NZ - 4), jax.random.fold_in(arg_keys[6], 1), 4, (NZ - 4) - 1).astype(jnp.int32)
    freqs = jnp.clip(jnp.exp(math.log(1.5) - 2.014903 * jax.random.uniform(arg_keys[7], (GROUPS, 2), jnp.float32) ** levels(arg_keys[7], (GROUPS, 2), ((0, 8),), -0.2, 0.2)), 0.2, 1.5)
    pml_width = jax.random.randint(arg_keys[8], (2,), 2, 8).astype(jnp.int32)
    design_blocks = draw_design_blocks(jax.random.fold_in(arg_keys[10], 71), 0)
    return {"efield": efield, "hfield": hfield, "fwd_dft": fwd_dft, "adj_dft": adj_dft, "permittivity": permittivity, "source_amp": source_amp, "source_plane": source_plane, "freqs": freqs, "pml_width": pml_width, "design_blocks": design_blocks}


courant = 0.5
absorb = 0.8

def ahead(field, axis):
    rest = lax.slice_in_dim(field, 1, field.shape[axis], axis=axis)
    zero = jnp.zeros_like(lax.slice_in_dim(field, 0, 1, axis=axis))
    return jnp.concatenate([rest, zero], axis) - field

def behind(field, axis):
    rest = lax.slice_in_dim(field, 0, field.shape[axis] - 1, axis=axis)
    zero = jnp.zeros_like(lax.slice_in_dim(field, 0, 1, axis=axis))
    return field - jnp.concatenate([zero, rest], axis)

def profile(count, width):
    cells = jnp.arange(count).astype(jnp.float32)
    dist = jnp.minimum(cells, count - 1.0 - cells)
    wide = width.astype(jnp.float32)
    return jnp.maximum(0.0, (wide - dist) / wide) ** 2

def reference(efield, hfield, fwd_dft, adj_dft, permittivity, source_amp, source_plane, freqs, pml_width, design_blocks):
    damp = jnp.exp(-absorb * (profile(NX, pml_width[0])[:, None] + profile(NY, pml_width[1])[None, :]))[:, :, None]
    coef = courant / permittivity
    xcell = jnp.arange(NX).astype(jnp.int32) // BS
    ycell = jnp.arange(NY).astype(jnp.int32) // BS
    cell_id = xcell[:, None] * (NY // BS) + ycell[None, :]
    mask = jnp.any(design_blocks[:, None, None] == cell_id[None], axis=0).astype(jnp.float32)[:, :, None]

    def one_group(g, total):
        ex, ey, ez = (efield[g, 0], efield[g, 1], efield[g, 2])
        hx, hy, hz = (hfield[g, 0], hfield[g, 1], hfield[g, 2])
        acc = adj_dft[g].astype(jnp.float32)
        omega = freqs[g]
        plane = (jnp.arange(NZ).astype(jnp.int32) == source_plane[g]).astype(jnp.float32)
        drive = source_amp[g][:, :, None] * plane[None, None, :]
        for step in range(STEPS):
            tval = jnp.float32(step + 1)
            hx = damp * (hx - courant * (ahead(ez, 1) - ahead(ey, 2)))
            hy = damp * (hy - courant * (ahead(ex, 2) - ahead(ez, 0)))
            hz = damp * (hz - courant * (ahead(ey, 0) - ahead(ex, 1)))
            ex = damp * (ex + coef * (behind(hz, 1) - behind(hy, 2)))
            ey = damp * (ey + coef * (behind(hx, 2) - behind(hz, 0)))
            ez = damp * (ez + coef * (behind(hy, 0) - behind(hx, 1)) + drive * jnp.sin(omega[0] * tval))
            efull = jnp.stack([ex, ey, ez])
            cosv = jnp.cos(omega * tval)[:, None, None, None, None]
            sinv = jnp.sin(omega * tval)[:, None, None, None, None]
            acc = jnp.stack([acc[:, 0] + cosv * efull, acc[:, 1] - sinv * efull], axis=1)
        term = lax.optimization_barrier(jnp.sum(fwd_dft[g].astype(jnp.float32) * acc, axis=(1, 2)))
        return total + term * mask[None]
    grad = lax.fori_loop(0, GROUPS, one_group, jnp.zeros((2, NX, NY, NZ), jnp.float32))
    squares = lax.optimization_barrier(jnp.sum(grad * grad, axis=(1, 2, 3)))
    count = jnp.float32(NB * BS * BS * NZ)
    return grad / jnp.sqrt(squares / count + 1e-05)[:, None, None, None]
```

```python
import functools

import jax
import jax.numpy as jnp
from jax import lax
from jax.experimental import pallas as pl
from jax.experimental.pallas import tpu as pltpu
from jax.sharding import PartitionSpec as P

BS = 8
MESH = pl.DeviceIdType.MESH
F32 = jnp.float32

courant = 0.5
absorb = 0.8

PLANES = 21
ROWS = 24
EX, EY, EZ, HX, HY, HZ, CO, DR = range(8)


def loop(low, count, unroll, step):
    assert count % unroll == 0

    def body(i, carry):
        for u in range(unroll):
            step(low + i * unroll + u)
        return carry

    lax.fori_loop(0, count // unroll, body, 0)


def kernel(
    e_hbm,
    h_hbm,
    fwd_hbm,
    adj_hbm,
    perm_hbm,
    amp_ref,
    plane_ref,
    freq_ref,
    pml_ref,
    blocks_ref,
    grad_hbm,
    scale_ref,
    field,
    damp,
    fwd,
    adj,
    trig,
    weights,
    term,
    landed,
    summed,
    row1,
    rows1,
    row2,
    rows2,
    load_sem,
    halo_send,
    halo_recv,
    red_send,
    red_recv,
    gat_send,
    gat_recv,
    s1_send,
    s1_recv,
    s2_send,
    s2_recv,
    out_sem,
):
    grp = lax.axis_index("grp")
    gx = lax.axis_index("gx")
    gy = lax.axis_index("gy")
    z_hi = grp // 4
    n_x = 8
    n_y = 8

    own = (pl.ds(2, 16), pl.ds(2, 16))
    loads = [
        pltpu.make_async_copy(e_hbm.at[0], field.at[(pl.ds(EX, 3), *own)], load_sem.at[0]),
        pltpu.make_async_copy(h_hbm.at[0], field.at[(pl.ds(HX, 3), *own)], load_sem.at[1]),
        pltpu.make_async_copy(perm_hbm, field.at[(CO, *own)], load_sem.at[2]),
        pltpu.make_async_copy(fwd_hbm.at[0], fwd, load_sem.at[3]),
        pltpu.make_async_copy(adj_hbm.at[0], adj, load_sem.at[4]),
    ]
    for copy in loads:
        copy.start()

    barrier = pltpu.get_barrier_semaphore()
    for d in range(1, 8):
        for axis, me in (("grp", grp), ("gx", gx), ("gy", gy)):
            pl.semaphore_signal(
                barrier, inc=1, device_id={axis: (me + d) % 8}, device_id_type=MESH
            )

    sides = [(dx, dy) for dx in (-1, 0, 1) for dy in (-1, 0, 1) if (dx, dy) != (0, 0)]

    def inside(dx, dy):
        ok = None
        for d, me, n in ((dx, gx, n_x), (dy, gy, n_y)):
            if d != 0:
                here = (me > 0) if d < 0 else (me < n - 1)
                ok = here if ok is None else jnp.logical_and(ok, here)
        return ok

    for dx, dy in sides:
        if dx != 0 and dy != 0:
            pl.semaphore_signal(
                barrier,
                inc=1,
                device_id={"gx": (gx + dx) % n_x, "gy": (gy + dy) % n_y},
                device_id_type=MESH,
            )

    @pl.when(gx == 0)
    def _():
        field[:, 0:2] = jnp.zeros((8, 2, ROWS, 128), F32)

    @pl.when(gx == n_x - 1)
    def _():
        field[:, 18:20] = jnp.zeros((8, 2, ROWS, 128), F32)

    @pl.when(gy == 0)
    def _():
        field[:, 0:20, 0:2, :] = jnp.zeros((8, 20, 2, 128), F32)

    @pl.when(gy == n_y - 1)
    def _():
        field[:, 0:20, 18:20, :] = jnp.zeros((8, 20, 2, 128), F32)

    total_x = n_x * 16
    total_y = n_y * 16

    def profile(cells, total, width):
        place = cells.astype(F32)
        dist = jnp.minimum(place, total - 1.0 - place)
        wide = jnp.full(cells.shape, width, jnp.int32).astype(F32)
        return jnp.maximum(0.0, (wide - dist) / wide) ** 2

    ys = gy * 16 - 2 + lax.broadcasted_iota(jnp.int32, (ROWS, 128), 0)
    prof_y = profile(ys, total_y, pml_ref[1])
    in_y = (ys >= 0) & (ys < total_y)

    def make_damp(p):
        xs = jnp.full((ROWS, 128), gx * 16 - 2 + p, jnp.int32)
        value = jnp.exp(-absorb * (profile(xs, total_x, pml_ref[0]) + prof_y))
        keep = in_y & (xs >= 0) & (xs < total_x)
        damp[p] = jnp.where(keep, value, 0.0)

    loop(0, 20, 4, make_damp)

    row_id = lax.broadcasted_iota(jnp.int32, (8, 128), 0)
    tval = (row_id % 2 + 1).astype(F32)
    omega = jnp.where(
        row_id < 2, jnp.full((8, 128), freq_ref[0, 0]), jnp.full((8, 128), freq_ref[0, 1])
    )
    trig[0:8] = jnp.cos(omega * tval)
    trig[8:16] = jnp.sin(omega * tval)

    eye = lax.broadcasted_iota(jnp.int32, (16, 16), 0) == lax.broadcasted_iota(
        jnp.int32, (16, 16), 1
    )
    lane16 = lax.broadcasted_iota(jnp.int32, (16, 128), 1)
    on_plane = lane16 == plane_ref[0]

    def make_drive(x):
        line = jnp.broadcast_to(amp_ref[0, pl.ds(x, 1), :], (16, 16))
        column = jnp.sum(jnp.where(eye, line, 0.0), axis=1, keepdims=True)
        field[DR, x + 2, pl.ds(2, 16), :] = jnp.where(
            on_plane, jnp.broadcast_to(column, (16, 128)), 0.0
        )

    loop(0, 16, 4, make_drive)

    loads[2].wait()

    def make_coef(p):
        field[CO, p, pl.ds(2, 16), :] = courant / field[CO, p, pl.ds(2, 16), :]

    loop(2, 16, 4, make_coef)

    loads[0].wait()
    loads[1].wait()

    pl.semaphore_wait(barrier, 25)

    def span(d, sending):
        if d == 0:
            return pl.ds(2, 16)
        if sending:
            return pl.ds(2, 2) if d < 0 else pl.ds(16, 2)
        return pl.ds(18, 2) if d < 0 else pl.ds(0, 2)

    def halo(i, dx, dy):
        return pltpu.make_async_remote_copy(
            src_ref=field.at[:, span(dx, True), span(dy, True), :],
            dst_ref=field.at[:, span(dx, False), span(dy, False), :],
            send_sem=halo_send.at[i],
            recv_sem=halo_recv.at[i],
            device_id={"gx": gx + dx, "gy": gy + dy},
            device_id_type=MESH,
        )

    for i, (dx, dy) in enumerate(sides):

        @pl.when(inside(dx, dy))
        def _(i=i, dx=dx, dy=dy):
            halo(i, dx, dy).start()

    loads[3].wait()
    loads[4].wait()

    blocks = blocks_ref[...]
    masks = []
    for bx in range(2):
        for by in range(2):
            cell = (gx * 2 + bx) * (total_y // BS) + gy * 2 + by
            hit = jnp.where(blocks == cell, 1.0, 0.0)
            masks.append(jnp.max(hit, axis=1, keepdims=True))
    upper = lax.broadcasted_iota(jnp.int32, (16, 128), 0) < 8

    def make_weights(bx):
        mask = jnp.where(
            upper,
            jnp.broadcast_to(masks[2 * bx], (16, 128)),
            jnp.broadcast_to(masks[2 * bx + 1], (16, 128)),
        )

        def step(x):
            for k in range(2):
                c1 = trig[pl.ds(2 * k, 1), :]
                c2 = trig[pl.ds(2 * k + 1, 1), :]
                s1 = trig[pl.ds(8 + 2 * k, 1), :]
                s2 = trig[pl.ds(8 + 2 * k + 1, 1), :]
                first = None
                for c in range(3):
                    fr = fwd[k, 0, c, x].astype(F32) * mask
                    fi = fwd[k, 1, c, x].astype(F32) * mask
                    ar = adj[k, 0, c, x].astype(F32)
                    ai = adj[k, 1, c, x].astype(F32)
                    part = fr * ar + fi * ai
                    first = part if first is None else first + part
                    weights[x, k * 7 + 1 + c, pl.ds(2, 16), :] = fr * c1 - fi * s1
                    weights[x, k * 7 + 4 + c, pl.ds(2, 16), :] = fr * c2 - fi * s2
                weights[x, k * 7, pl.ds(2, 16), :] = first

        loop(bx * 8, 8, 1, step)

    make_weights(0)
    make_weights(1)

    for i, (dx, dy) in enumerate(sides):

        @pl.when(inside(dx, dy))
        def _(i=i, dx=dx, dy=dy):
            halo(i, dx, dy).wait_send()

    for i, (dx, dy) in enumerate(sides):

        @pl.when(inside(-dx, -dy))
        def _(i=i, dx=dx, dy=dy):
            halo(i, dx, dy).wait_recv()

    lane = lax.broadcasted_iota(jnp.int32, (ROWS, 128), 1)
    not_last = lane < 127
    not_first = lane > 0

    def ahead_z(v):
        return jnp.where(not_last, pltpu.roll(v, 127, 1), 0.0) - v

    def behind_z(v):
        return v - jnp.where(not_first, pltpu.roll(v, 1, 1), 0.0)

    def ahead_y(v):
        return pltpu.roll(v, ROWS - 1, 0) - v

    def behind_y(v):
        return v - pltpu.roll(v, 1, 0)

    def magnetic(p):
        ex, ey, ez = field[EX, p], field[EY, p], field[EZ, p]
        ey_dx = field[EY, p + 1] - ey
        ez_dx = field[EZ, p + 1] - ez
        d = damp[p]
        field[HX, p] = d * (field[HX, p] - courant * (ahead_y(ez) - ahead_z(ey)))
        field[HY, p] = d * (field[HY, p] - courant * (ahead_z(ex) - ez_dx))
        field[HZ, p] = d * (field[HZ, p] - courant * (ey_dx - ahead_y(ex)))

    def electric(p, sine):
        hx, hy, hz = field[HX, p], field[HY, p], field[HZ, p]
        hy_dx = hy - field[HY, p - 1]
        hz_dx = hz - field[HZ, p - 1]
        d = damp[p]
        co = field[CO, p]
        ex = d * (field[EX, p] + co * (behind_y(hz) - behind_z(hy)))
        ey = d * (field[EY, p] + co * (behind_z(hx) - hz_dx))
        ez = d * (field[EZ, p] + co * (hy_dx - behind_y(hx)) + field[DR, p] * sine)
        return ex, ey, ez

    def electric1(p):
        ex, ey, ez = electric(p, trig[pl.ds(8, 1), :])
        field[EX, p] = ex
        field[EY, p] = ey
        field[EZ, p] = ez

    def electric2(p):
        new = electric(p, trig[pl.ds(9, 1), :])
        old = (field[EX, p], field[EY, p], field[EZ, p])
        x = p - 2
        for k in range(2):
            value = weights[x, k * 7]
            for c in range(3):
                value = value + weights[x, k * 7 + 1 + c] * old[c]
                value = value + weights[x, k * 7 + 4 + c] * new[c]
            term[k, x] = value

    loop(0, 19, 1, magnetic)
    loop(1, 18, 3, electric1)
    loop(1, 17, 1, magnetic)
    loop(2, 16, 2, electric2)

    def piece(j):
        return term.at[j // 4, pl.ds((j % 4) * 4, 4), pl.ds(2, 16), :]

    def reduce_copy(to):
        return pltpu.make_async_remote_copy(
            src_ref=piece(to),
            dst_ref=landed.at[grp],
            send_sem=red_send,
            recv_sem=red_recv,
            device_id={"grp": to},
            device_id_type=MESH,
        )

    for d in (4, 6, 5, 7, 2, 1, 3):
        reduce_copy((grp + d) % 8).start()
    landed[grp] = term[grp // 4, pl.ds((grp % 4) * 4, 4), pl.ds(2, 16), :]
    seven = landed.at[pl.ds(0, 7)]
    pltpu.make_async_copy(seven, seven, red_recv).wait()

    total = landed[0]
    for j in range(1, 8):
        total = total + landed[j]
    summed[grp] = total
    square = jnp.sum(total * total, axis=0)
    line = jnp.sum(square, axis=0, keepdims=True)

    me1 = (grp % 4) * 8 + gy
    me2 = z_hi * 8 + gx
    row1[...] = line
    rows1[pl.ds(me1, 1), :] = line
    for d in range(1, 32):
        to = (me1 + d) % 32
        pltpu.make_async_remote_copy(
            src_ref=row1,
            dst_ref=rows1.at[pl.ds(me1, 1)],
            send_sem=s1_send,
            recv_sem=s1_recv,
            device_id={"grp": z_hi * 4 + to // 8, "gy": to % 8},
            device_id_type=MESH,
        ).start()

    def gather_copy(to):
        return pltpu.make_async_remote_copy(
            src_ref=summed.at[grp],
            dst_ref=summed.at[grp],
            send_sem=gat_send,
            recv_sem=gat_recv,
            device_id={"grp": to},
            device_id_type=MESH,
        )

    for d in (4, 6, 5, 7, 2, 1, 3):
        gather_copy((grp + d) % 8).start()

    some = rows1.at[pl.ds(0, 31)]
    pltpu.make_async_copy(some, some, s1_recv).wait()
    line = jnp.sum(rows1[...], axis=0, keepdims=True)
    row2[...] = line
    rows2[pl.ds(me2, 1), :] = line
    for d in range(1, 16):
        to = (me2 + d) % 16
        pltpu.make_async_remote_copy(
            src_ref=row2,
            dst_ref=rows2.at[pl.ds(me2, 1)],
            send_sem=s2_send,
            recv_sem=s2_recv,
            device_id={"grp": (to // 8) * 4 + grp % 4, "gx": to % 8},
            device_id_type=MESH,
        ).start()

    seven = summed.at[pl.ds(0, 7)]
    pltpu.make_async_copy(seven, seven, gat_recv).wait()
    out = pltpu.make_async_copy(summed, grad_hbm, out_sem)
    out.start()

    few = rows2.at[pl.ds(0, 15)]
    pltpu.make_async_copy(few, few, s2_recv).wait()
    count = float(128 * BS * BS * 128)
    for k in range(2):
        squares = jnp.sum(rows2[8 * k : 8 * k + 8], axis=0, keepdims=True)
        squares = jnp.sum(squares, axis=1, keepdims=True)
        value = lax.rsqrt(squares / count + 1e-05)
        scale_ref[k] = jnp.broadcast_to(value, (8, 128))

    out.wait()
    sent = landed.at[pl.ds(0, 7)]
    pltpu.make_async_copy(sent, sent, red_send).wait()
    pltpu.make_async_copy(seven, seven, gat_send).wait()
    pltpu.make_async_copy(some, some, s1_send).wait()
    pltpu.make_async_copy(few, few, s2_send).wait()


def body(
    efield,
    hfield,
    fwd_dft,
    adj_dft,
    permittivity,
    source_amp,
    source_plane,
    freqs,
    pml_width,
    design_blocks,
):
    hbm = pl.BlockSpec(memory_space=pl.ANY)
    vmem = pl.BlockSpec(memory_space=pltpu.VMEM)
    smem = pl.BlockSpec(memory_space=pltpu.SMEM)
    dma = pltpu.SemaphoreType.DMA
    grad, scale = pl.pallas_call(
        kernel,
        out_shape=(
            jax.ShapeDtypeStruct((8, 4, 16, 128), F32),
            jax.ShapeDtypeStruct((2, 8, 128), F32),
        ),
        in_specs=[hbm, hbm, hbm, hbm, hbm, vmem, smem, smem, smem, vmem],
        out_specs=(hbm, vmem),
        scratch_shapes=[
            pltpu.VMEM((8, PLANES, ROWS, 128), F32),
            pltpu.VMEM((20, ROWS, 128), F32),
            pltpu.VMEM((2, 2, 3, 16, 16, 128), jnp.bfloat16),
            pltpu.VMEM((2, 2, 3, 16, 16, 128), jnp.bfloat16),
            pltpu.VMEM((16, 128), F32),
            pltpu.VMEM((16, 14, ROWS, 128), F32),
            pltpu.VMEM((2, 16, ROWS, 128), F32),
            pltpu.VMEM((8, 4, 16, 128), F32),
            pltpu.VMEM((8, 4, 16, 128), F32),
            pltpu.VMEM((1, 128), F32),
            pltpu.VMEM((32, 128), F32),
            pltpu.VMEM((1, 128), F32),
            pltpu.VMEM((16, 128), F32),
            dma((5,)),
            dma((8,)),
            dma((8,)),
            dma,
            dma,
            dma,
            dma,
            dma,
            dma,
            dma,
            dma,
            dma,
        ],
        compiler_params=pltpu.CompilerParams(
            collective_id=0, has_side_effects=True, vmem_limit_bytes=40 * 1024 * 1024
        ),
        name="adjoint",
    )(
        efield,
        hfield,
        fwd_dft,
        adj_dft,
        permittivity,
        source_amp,
        source_plane,
        freqs,
        pml_width,
        design_blocks[None, :],
    )
    return grad.reshape(2, 16, 16, 128) * scale[:, :1, None, :]


def solution(mesh):
    in_specs = (
        P("grp", None, "gx", "gy", None),
        P("grp", None, "gx", "gy", None),
        P("grp", None, None, None, "gx", "gy", None),
        P("grp", None, None, None, "gx", "gy", None),
        P("gx", "gy", None),
        P("grp", "gx", "gy"),
        P("grp"),
        P("grp", None),
        P(),
        P(),
    )
    out_specs = P(None, "gx", "gy", None)
    return jax.shard_map(body, mesh=mesh, in_specs=in_specs, out_specs=out_specs, check_vma=False)
```

```python
import functools

import jax
import jax.numpy as jnp
from jax import lax
from jax.experimental import pallas as pl
from jax.experimental.pallas import tpu as pltpu
from jax.sharding import PartitionSpec as P

BS = 8
MESH = pl.DeviceIdType.MESH
F32 = jnp.float32

courant = 0.5
absorb = 0.8

PLANES = 21
ROWS = 24
EX, EY, EZ, HX, HY, HZ, CO, DR = range(8)


def loop(low, count, unroll, step):
    assert count % unroll == 0

    def body(i, carry):
        for u in range(unroll):
            step(low + i * unroll + u)
        return carry

    lax.fori_loop(0, count // unroll, body, 0)


def kernel(
    e_hbm,
    h_hbm,
    fwd_hbm,
    adj_hbm,
    perm_hbm,
    amp_hbm,
    plane_ref,
    freq_hbm,
    pml_hbm,
    blocks_hbm,
    grad_hbm,
    scale_ref,
    field,
    damp,
    fwd,
    adj,
    trig,
    weights,
    term,
    landed,
    summed,
    row1,
    rows1,
    row2,
    rows2,
    amp_ref,
    freq_ref,
    pml_ref,
    blocks_ref,
    load_sem,
    halo_send,
    halo_recv,
    red_send,
    red_recv,
    gat_send,
    gat_recv,
    s1_send,
    s1_recv,
    s2_send,
    s2_recv,
    out_sem,
):
    grp = lax.axis_index("grp")
    gx = lax.axis_index("gx")
    gy = lax.axis_index("gy")
    z_hi = grp // 4
    n_x = 8
    n_y = 8

    sides = [(dx, dy) for dx in (-1, 0, 1) for dy in (-1, 0, 1) if (dx, dy) != (0, 0)]
    barrier = pltpu.get_barrier_semaphore()

    def greet(device):
        pl.semaphore_signal(barrier, inc=1, device_id=device, device_id_type=MESH)

    for dx, dy in sides:
        device = {}
        if dx != 0:
            device["gx"] = (gx + dx) % n_x
        if dy != 0:
            device["gy"] = (gy + dy) % n_y
        greet(device)

    own = (pl.ds(2, 16), pl.ds(2, 16))
    loads = [
        pltpu.make_async_copy(e_hbm.at[0], field.at[(pl.ds(EX, 3), *own)], load_sem.at[0]),
        pltpu.make_async_copy(h_hbm.at[0], field.at[(pl.ds(HX, 3), *own)], load_sem.at[1]),
        pltpu.make_async_copy(perm_hbm, field.at[(CO, *own)], load_sem.at[2]),
        pltpu.make_async_copy(fwd_hbm.at[0], fwd, load_sem.at[3]),
        pltpu.make_async_copy(adj_hbm.at[0], adj, load_sem.at[4]),
        pltpu.make_async_copy(pml_hbm, pml_ref, load_sem.at[5]),
        pltpu.make_async_copy(freq_hbm, freq_ref, load_sem.at[6]),
        pltpu.make_async_copy(amp_hbm, amp_ref, load_sem.at[7]),
        pltpu.make_async_copy(blocks_hbm, blocks_ref, load_sem.at[8]),
    ]
    for i in (5, 2, 7, 0, 1, 6, 3, 4, 8):
        loads[i].start()

    for d in range(4, 8):
        greet({"grp": (grp + d) % 8})
    for d in range(1, 4):
        greet({"grp": (grp + d) % 8})
    for d in range(2, 7):
        greet({"gx": (gx + d) % 8})
        greet({"gy": (gy + d) % 8})

    def inside(dx, dy):
        ok = None
        for d, me, n in ((dx, gx, n_x), (dy, gy, n_y)):
            if d != 0:
                here = (me > 0) if d < 0 else (me < n - 1)
                ok = here if ok is None else jnp.logical_and(ok, here)
        return ok

    @pl.when(gx == 0)
    def _():
        field[:, 0:2] = jnp.zeros((8, 2, ROWS, 128), F32)

    @pl.when(gx == n_x - 1)
    def _():
        field[:, 18:20] = jnp.zeros((8, 2, ROWS, 128), F32)

    @pl.when(gy == 0)
    def _():
        field[:, 0:20, 0:2, :] = jnp.zeros((8, 20, 2, 128), F32)

    @pl.when(gy == n_y - 1)
    def _():
        field[:, 0:20, 18:20, :] = jnp.zeros((8, 20, 2, 128), F32)

    total_x = n_x * 16
    total_y = n_y * 16

    def profile(cells, total, width):
        place = cells.astype(F32)
        dist = jnp.minimum(place, total - 1.0 - place)
        wide = jnp.full(cells.shape, width, jnp.int32).astype(F32)
        return jnp.maximum(0.0, (wide - dist) / wide) ** 2

    loads[5].wait()
    ys = gy * 16 - 2 + lax.broadcasted_iota(jnp.int32, (ROWS, 128), 0)
    prof_y = profile(ys, total_y, pml_ref[1])
    in_y = (ys >= 0) & (ys < total_y)

    def make_damp(p):
        xs = jnp.full((ROWS, 128), gx * 16 - 2 + p, jnp.int32)
        value = jnp.exp(-absorb * (profile(xs, total_x, pml_ref[0]) + prof_y))
        keep = in_y & (xs >= 0) & (xs < total_x)
        damp[p] = jnp.where(keep, value, 0.0)

    loop(0, 20, 4, make_damp)

    eye = lax.broadcasted_iota(jnp.int32, (16, 16), 0) == lax.broadcasted_iota(
        jnp.int32, (16, 16), 1
    )
    loads[7].wait()
    lane16 = lax.broadcasted_iota(jnp.int32, (16, 128), 1)
    on_plane = lane16 == plane_ref[0]

    def make_drive(x):
        line = jnp.broadcast_to(amp_ref[0, pl.ds(x, 1), :], (16, 16))
        column = jnp.sum(jnp.where(eye, line, 0.0), axis=1, keepdims=True)
        field[DR, x + 2, pl.ds(2, 16), :] = jnp.where(
            on_plane, jnp.broadcast_to(column, (16, 128)), 0.0
        )

    loop(0, 16, 4, make_drive)

    loads[2].wait()

    def make_coef(p):
        field[CO, p, pl.ds(2, 16), :] = courant / field[CO, p, pl.ds(2, 16), :]

    loop(2, 16, 4, make_coef)

    loads[0].wait()
    loads[1].wait()

    pl.semaphore_wait(barrier, 25)

    def span(d, sending):
        if d == 0:
            return pl.ds(2, 16)
        if sending:
            return pl.ds(2, 2) if d < 0 else pl.ds(16, 2)
        return pl.ds(18, 2) if d < 0 else pl.ds(0, 2)

    def halo(i, dx, dy):
        return pltpu.make_async_remote_copy(
            src_ref=field.at[:, span(dx, True), span(dy, True), :],
            dst_ref=field.at[:, span(dx, False), span(dy, False), :],
            send_sem=halo_send.at[i],
            recv_sem=halo_recv.at[i],
            device_id={"gx": gx + dx, "gy": gy + dy},
            device_id_type=MESH,
        )

    for i, (dx, dy) in enumerate(sides):

        @pl.when(inside(dx, dy))
        def _(i=i, dx=dx, dy=dy):
            halo(i, dx, dy).start()

    loads[6].wait()
    row_id = lax.broadcasted_iota(jnp.int32, (8, 128), 0)
    tval = (row_id % 2 + 1).astype(F32)
    omega = jnp.where(
        row_id < 2, jnp.full((8, 128), freq_ref[0, 0]), jnp.full((8, 128), freq_ref[0, 1])
    )
    trig[0:8] = jnp.cos(omega * tval)
    trig[8:16] = jnp.sin(omega * tval)

    loads[8].wait()
    loads[3].wait()
    loads[4].wait()

    blocks = blocks_ref[...]
    masks = []
    for bx in range(2):
        for by in range(2):
            cell = (gx * 2 + bx) * (total_y // BS) + gy * 2 + by
            hit = jnp.where(blocks == cell, 1.0, 0.0)
            masks.append(jnp.max(hit, axis=1, keepdims=True))
    upper = lax.broadcasted_iota(jnp.int32, (16, 128), 0) < 8

    def make_weights(bx):
        mask = jnp.where(
            upper,
            jnp.broadcast_to(masks[2 * bx], (16, 128)),
            jnp.broadcast_to(masks[2 * bx + 1], (16, 128)),
        )

        def step(x):
            for k in range(2):
                c1 = trig[pl.ds(2 * k, 1), :]
                c2 = trig[pl.ds(2 * k + 1, 1), :]
                s1 = trig[pl.ds(8 + 2 * k, 1), :]
                s2 = trig[pl.ds(8 + 2 * k + 1, 1), :]
                first = None
                for c in range(3):
                    fr = fwd[k, 0, c, x].astype(F32) * mask
                    fi = fwd[k, 1, c, x].astype(F32) * mask
                    ar = adj[k, 0, c, x].astype(F32)
                    ai = adj[k, 1, c, x].astype(F32)
                    part = fr * ar + fi * ai
                    first = part if first is None else first + part
                    weights[x, k * 7 + 1 + c, pl.ds(2, 16), :] = fr * c1 - fi * s1
                    weights[x, k * 7 + 4 + c, pl.ds(2, 16), :] = fr * c2 - fi * s2
                weights[x, k * 7, pl.ds(2, 16), :] = first

        loop(bx * 8, 8, 1, step)

    make_weights(0)
    make_weights(1)

    for i, (dx, dy) in enumerate(sides):

        @pl.when(inside(dx, dy))
        def _(i=i, dx=dx, dy=dy):
            halo(i, dx, dy).wait_send()

    for i, (dx, dy) in enumerate(sides):

        @pl.when(inside(-dx, -dy))
        def _(i=i, dx=dx, dy=dy):
            halo(i, dx, dy).wait_recv()

    lane = lax.broadcasted_iota(jnp.int32, (ROWS, 128), 1)
    not_last = lane < 127
    not_first = lane > 0

    def ahead_z(v):
        return jnp.where(not_last, pltpu.roll(v, 127, 1), 0.0) - v

    def behind_z(v):
        return v - jnp.where(not_first, pltpu.roll(v, 1, 1), 0.0)

    def ahead_y(v):
        return pltpu.roll(v, ROWS - 1, 0) - v

    def behind_y(v):
        return v - pltpu.roll(v, 1, 0)

    def magnetic(p, e, ahead, h):
        d = damp[p]
        ex, ey, ez = e
        hx = d * (h[0] - courant * (ahead_y(ez) - ahead_z(ey)))
        hy = d * (h[1] - courant * (ahead_z(ex) - (ahead[2] - ez)))
        hz = d * (h[2] - courant * ((ahead[1] - ey) - ahead_y(ex)))
        return hx, hy, hz

    def electric(p, h, behind, e, sine):
        d = damp[p]
        co = field[CO, p]
        hx, hy, hz = h
        ex = d * (e[0] + co * (behind_y(hz) - behind_z(hy)))
        ey = d * (e[1] + co * (behind_z(hx) - (hz - behind[2])))
        ez = d * (e[2] + co * ((hy - behind[1]) - behind_y(hx)) + field[DR, p] * sine)
        return ex, ey, ez

    sine1 = trig[pl.ds(8, 1), :]
    sine2 = trig[pl.ds(9, 1), :]

    def read(first, p):
        return tuple(field[first + c, p] for c in range(3))

    def reduce_copy(to):
        return pltpu.make_async_remote_copy(
            src_ref=term.at[to // 4, pl.ds((to % 4) * 4, 4), pl.ds(2, 16), :],
            dst_ref=landed.at[grp],
            send_sem=red_send,
            recv_sem=red_recv,
            device_id={"grp": to},
            device_id_type=MESH,
        )

    def send_quarter(q):
        for to in (q, q + 4):

            @pl.when(grp != to)
            def _():
                reduce_copy(to).start()

            @pl.when(grp == to)
            def _():
                landed[to] = term[to // 4, 4 * (to % 4) : 4 * (to % 4) + 4, 2:18, :]

    e0 = read(EX, 0)
    h1 = e1 = h2 = None
    for p in range(19):
        e0_next = read(EX, p + 1)
        h1_last, e1_last, h2_last = h1, e1, h2
        h1 = magnetic(p, e0, e0_next, read(HX, p))
        if p >= 1:
            e1 = electric(p, h1, h1_last, e0, sine1)
        if p >= 2:
            h2 = magnetic(p - 1, e1_last, e1, h1_last)
        if p >= 3:
            e2 = electric(p - 1, h2, h2_last, e1_last, sine2)
            x = p - 3
            for k in range(2):
                value = weights[x, k * 7]
                for c in range(3):
                    value = value + weights[x, k * 7 + 1 + c] * e1_last[c]
                    value = value + weights[x, k * 7 + 4 + c] * e2[c]
                term[k, x] = value
            if x % 4 == 3:
                send_quarter(x // 4)
        e0 = e0_next

    seven = landed.at[pl.ds(0, 7)]
    pltpu.make_async_copy(seven, seven, red_recv).wait()

    total = landed[0]
    for j in range(1, 8):
        total = total + landed[j]
    summed[grp] = total
    square = jnp.sum(total * total, axis=0)
    line = jnp.sum(square, axis=0, keepdims=True)

    me1 = (grp % 4) * 8 + gy
    me2 = z_hi * 8 + gx
    row1[...] = line
    rows1[pl.ds(me1, 1), :] = line
    for d in range(1, 32):
        to = (me1 + d) % 32
        pltpu.make_async_remote_copy(
            src_ref=row1,
            dst_ref=rows1.at[pl.ds(me1, 1)],
            send_sem=s1_send,
            recv_sem=s1_recv,
            device_id={"grp": z_hi * 4 + to // 8, "gy": to % 8},
            device_id_type=MESH,
        ).start()

    def gather_copy(to):
        return pltpu.make_async_remote_copy(
            src_ref=summed.at[grp],
            dst_ref=summed.at[grp],
            send_sem=gat_send,
            recv_sem=gat_recv,
            device_id={"grp": to},
            device_id_type=MESH,
        )

    for d in (4, 6, 5, 7, 2, 1, 3):
        gather_copy((grp + d) % 8).start()

    some = rows1.at[pl.ds(0, 31)]
    pltpu.make_async_copy(some, some, s1_recv).wait()
    line = jnp.sum(rows1[...], axis=0, keepdims=True)
    row2[...] = line
    rows2[pl.ds(me2, 1), :] = line
    for d in range(1, 16):
        to = (me2 + d) % 16
        pltpu.make_async_remote_copy(
            src_ref=row2,
            dst_ref=rows2.at[pl.ds(me2, 1)],
            send_sem=s2_send,
            recv_sem=s2_recv,
            device_id={"grp": (to // 8) * 4 + grp % 4, "gx": to % 8},
            device_id_type=MESH,
        ).start()

    seven = summed.at[pl.ds(0, 7)]
    pltpu.make_async_copy(seven, seven, gat_recv).wait()
    out = pltpu.make_async_copy(summed, grad_hbm, out_sem)
    out.start()

    few = rows2.at[pl.ds(0, 15)]
    pltpu.make_async_copy(few, few, s2_recv).wait()
    count = float(128 * BS * BS * 128)
    for k in range(2):
        squares = jnp.sum(rows2[8 * k : 8 * k + 8], axis=0, keepdims=True)
        squares = jnp.sum(squares, axis=1, keepdims=True)
        value = lax.rsqrt(squares / count + 1e-05)
        scale_ref[k] = jnp.broadcast_to(value, (8, 128))

    out.wait()
    sent = landed.at[pl.ds(0, 7)]
    pltpu.make_async_copy(sent, sent, red_send).wait()
    pltpu.make_async_copy(seven, seven, gat_send).wait()
    pltpu.make_async_copy(some, some, s1_send).wait()
    pltpu.make_async_copy(few, few, s2_send).wait()


def body(
    efield,
    hfield,
    fwd_dft,
    adj_dft,
    permittivity,
    source_amp,
    source_plane,
    freqs,
    pml_width,
    design_blocks,
):
    hbm = pl.BlockSpec(memory_space=pltpu.HBM)
    def pin(value):
        return pltpu.with_memory_space_constraint(value, pltpu.HBM)

    vmem = pl.BlockSpec(memory_space=pltpu.VMEM)
    dma = pltpu.SemaphoreType.DMA
    grad, scale = pl.pallas_call(
        kernel,
        out_shape=(
            jax.ShapeDtypeStruct((8, 4, 16, 128), F32),
            jax.ShapeDtypeStruct((2, 8, 128), F32),
        ),
        in_specs=[hbm] * 6 + [pl.BlockSpec(memory_space=pltpu.SMEM)] + [hbm] * 3,
        out_specs=(pl.BlockSpec(memory_space=pl.ANY), vmem),
        scratch_shapes=[
            pltpu.VMEM((8, PLANES, ROWS, 128), F32),
            pltpu.VMEM((20, ROWS, 128), F32),
            pltpu.VMEM((2, 2, 3, 16, 16, 128), jnp.bfloat16),
            pltpu.VMEM((2, 2, 3, 16, 16, 128), jnp.bfloat16),
            pltpu.VMEM((16, 128), F32),
            pltpu.VMEM((16, 14, ROWS, 128), F32),
            pltpu.VMEM((2, 16, ROWS, 128), F32),
            pltpu.VMEM((8, 4, 16, 128), F32),
            pltpu.VMEM((8, 4, 16, 128), F32),
            pltpu.VMEM((1, 128), F32),
            pltpu.VMEM((32, 128), F32),
            pltpu.VMEM((1, 128), F32),
            pltpu.VMEM((16, 128), F32),
            pltpu.VMEM((1, 16, 16), F32),
            pltpu.SMEM((1, 2), F32),
            pltpu.SMEM((2,), jnp.int32),
            pltpu.VMEM((1, 128), jnp.int32),
            dma((9,)),
            dma((8,)),
            dma((8,)),
            dma,
            dma,
            dma,
            dma,
            dma,
            dma,
            dma,
            dma,
            dma,
        ],
        compiler_params=pltpu.CompilerParams(
            collective_id=0, has_side_effects=True, vmem_limit_bytes=40 * 1024 * 1024
        ),
        name="adjoint",
    )(
        *map(pin, (efield, hfield, fwd_dft, adj_dft, permittivity, source_amp)),
        source_plane,
        *map(pin, (freqs, pml_width, design_blocks[None, :])),
    )
    return grad.reshape(2, 16, 16, 128) * scale[:, :1, None, :]


def solution(mesh):
    in_specs = (
        P("grp", None, "gx", "gy", None),
        P("grp", None, "gx", "gy", None),
        P("grp", None, None, None, "gx", "gy", None),
        P("grp", None, None, None, "gx", "gy", None),
        P("gx", "gy", None),
        P("grp", "gx", "gy"),
        P("grp"),
        P("grp", None),
        P(),
        P(),
    )
    out_specs = P(None, "gx", "gy", None)
    return jax.shard_map(body, mesh=mesh, in_specs=in_specs, out_specs=out_specs, check_vma=False)
```

```python
import functools

import jax
import jax.numpy as jnp
from jax import lax
from jax.experimental import pallas as pl
from jax.experimental.pallas import tpu as pltpu
from jax.sharding import PartitionSpec as P

BS = 8
MESH = pl.DeviceIdType.MESH
F32 = jnp.float32

courant = 0.5
absorb = 0.8

PLANES = 21
ROWS = 24
EX, EY, EZ, HX, HY, HZ, CO, DR = range(8)


def loop(low, count, unroll, step):
    assert count % unroll == 0

    def body(i, carry):
        for u in range(unroll):
            step(low + i * unroll + u)
        return carry

    lax.fori_loop(0, count // unroll, body, 0)


def kernel(
    e_hbm,
    h_hbm,
    fwd_hbm,
    adj_hbm,
    perm_hbm,
    amp_hbm,
    plane_ref,
    freq_hbm,
    pml_hbm,
    blocks_hbm,
    grad_hbm,
    scale_ref,
    field,
    damp,
    fwd,
    adj,
    trig,
    weights,
    term,
    landed,
    summed,
    row1,
    rows1,
    row2,
    rows2,
    amp_ref,
    freq_ref,
    pml_ref,
    blocks_ref,
    load_sem,
    halo_send,
    halo_recv,
    red_send,
    red_recv,
    gat_send,
    gat_recv,
    s1_send,
    s1_recv,
    s2_send,
    s2_recv,
    out_sem,
):
    grp = lax.axis_index("grp")
    gx = lax.axis_index("gx")
    gy = lax.axis_index("gy")
    z_hi = grp // 4
    n_x = 8
    n_y = 8

    sides = [(dx, dy) for dx in (-1, 0, 1) for dy in (-1, 0, 1) if (dx, dy) != (0, 0)]
    barrier = pltpu.get_barrier_semaphore()

    def greet(device):
        pl.semaphore_signal(barrier, inc=1, device_id=device, device_id_type=MESH)

    for dx, dy in sides:
        device = {}
        if dx != 0:
            device["gx"] = (gx + dx) % n_x
        if dy != 0:
            device["gy"] = (gy + dy) % n_y
        greet(device)

    own = (pl.ds(2, 16), pl.ds(2, 16))
    loads = [
        pltpu.make_async_copy(e_hbm.at[0], field.at[(pl.ds(EX, 3), *own)], load_sem.at[0]),
        pltpu.make_async_copy(h_hbm.at[0], field.at[(pl.ds(HX, 3), *own)], load_sem.at[1]),
        pltpu.make_async_copy(perm_hbm, field.at[(CO, *own)], load_sem.at[2]),
        pltpu.make_async_copy(fwd_hbm.at[0], fwd, load_sem.at[3]),
        pltpu.make_async_copy(adj_hbm.at[0], adj, load_sem.at[4]),
        pltpu.make_async_copy(pml_hbm, pml_ref, load_sem.at[5]),
        pltpu.make_async_copy(freq_hbm, freq_ref, load_sem.at[6]),
        pltpu.make_async_copy(amp_hbm, amp_ref, load_sem.at[7]),
        pltpu.make_async_copy(blocks_hbm, blocks_ref, load_sem.at[8]),
    ]
    for i in (5, 2, 7, 0, 1, 6, 3, 4, 8):
        loads[i].start()

    for d in range(4, 8):
        greet({"grp": (grp + d) % 8})
    for d in range(1, 4):
        greet({"grp": (grp + d) % 8})
    for d in range(2, 7):
        greet({"gx": (gx + d) % 8})
        greet({"gy": (gy + d) % 8})

    def inside(dx, dy):
        ok = None
        for d, me, n in ((dx, gx, n_x), (dy, gy, n_y)):
            if d != 0:
                here = (me > 0) if d < 0 else (me < n - 1)
                ok = here if ok is None else jnp.logical_and(ok, here)
        return ok

    pl.semaphore_wait(barrier, 25)

    def pick(d, wide):
        if d == 0:
            return pl.ds(0, 16), pl.ds(2, 16)
        if d > 0:
            return pl.ds(16 - wide, wide), pl.ds(2 - wide, wide)
        return pl.ds(0, wide), pl.ds(18, wide)

    e_arg, h_arg = e_hbm.at[0], h_hbm.at[0]
    parts = {
        (1, 0): [(e_arg, EX, 0, 3, 2, 0), (h_arg, HX, 1, 2, 2, 0), (h_arg, HX, 0, 1, 1, 0)],
        (-1, 0): [(e_arg, EX, 1, 2, 2, 0), (h_arg, HX, 0, 3, 1, 0), (e_arg, EX, 0, 1, 1, 0)],
        (0, 1): [(e_arg, EX, 0, 3, 0, 2), (h_arg, HX, 0, 3, 0, 2)],
        (0, -1): [(e_arg, EX, 0, 3, 0, 2), (h_arg, HX, 0, 3, 0, 1)],
        (1, 1): [(e_arg, EX, 0, 3, 1, 1), (h_arg, HX, 0, 3, 1, 1)],
        (1, -1): [(e_arg, EX, 0, 3, 2, 2), (h_arg, HX, 0, 3, 1, 1)],
        (-1, 1): [(e_arg, EX, 0, 3, 2, 2), (h_arg, HX, 0, 3, 1, 1)],
        (-1, -1): [(e_arg, EX, 0, 3, 1, 1)],
    }

    def halo(dx, dy):
        copies = []
        for i, (source, base, first, many, wide_x, wide_y) in enumerate(parts[dx, dy]):
            from_x, to_x = pick(dx, wide_x)
            from_y, to_y = pick(dy, wide_y)
            slot = 3 * sides.index((dx, dy)) + i
            copies.append(
                pltpu.make_async_remote_copy(
                    src_ref=source.at[pl.ds(first, many), from_x, from_y, :],
                    dst_ref=field.at[pl.ds(base + first, many), to_x, to_y, :],
                    send_sem=halo_send.at[slot],
                    recv_sem=halo_recv.at[slot],
                    device_id={"gx": gx + dx, "gy": gy + dy},
                    device_id_type=MESH,
                )
            )
        return copies

    def aux(dx, dy):
        from_x, to_x = pick(dx, 1)
        from_y, to_y = pick(dy, 1)
        slot = 24 + sides.index((dx, dy))
        inner_x = pl.ds(from_x.start + 2, from_x.size)
        inner_y = pl.ds(from_y.start + 2, from_y.size)
        return pltpu.make_async_remote_copy(
            src_ref=field.at[pl.ds(CO, 2), inner_x, inner_y, :],
            dst_ref=field.at[pl.ds(CO, 2), to_x, to_y, :],
            send_sem=halo_send.at[slot],
            recv_sem=halo_recv.at[slot],
            device_id={"gx": gx + dx, "gy": gy + dy},
            device_id_type=MESH,
        )

    order = [(0, 1), (0, -1), (1, 0), (-1, 0), (1, -1), (-1, 1), (1, 1), (-1, -1)]
    aux_order = [side for side in order if side not in ((1, 1), (-1, -1))]

    for dx, dy in order:

        @pl.when(inside(dx, dy))
        def _(dx=dx, dy=dy):
            for copy in halo(dx, dy):
                copy.start()

    def start_aux():
        for dx, dy in aux_order:

            @pl.when(inside(dx, dy))
            def _(dx=dx, dy=dy):
                aux(dx, dy).start()

    @pl.when(gx == 0)
    def _():
        field[:, 0:2] = jnp.zeros((8, 2, ROWS, 128), F32)

    @pl.when(gx == n_x - 1)
    def _():
        field[:, 18:20] = jnp.zeros((8, 2, ROWS, 128), F32)

    @pl.when(gy == 0)
    def _():
        field[:, 0:20, 0:2, :] = jnp.zeros((8, 20, 2, 128), F32)

    @pl.when(gy == n_y - 1)
    def _():
        field[:, 0:20, 18:20, :] = jnp.zeros((8, 20, 2, 128), F32)

    eye = lax.broadcasted_iota(jnp.int32, (16, 16), 0) == lax.broadcasted_iota(
        jnp.int32, (16, 16), 1
    )
    loads[7].wait()
    lane16 = lax.broadcasted_iota(jnp.int32, (16, 128), 1)
    on_plane = lane16 == plane_ref[0]

    def make_drive(x):
        line = jnp.broadcast_to(amp_ref[0, pl.ds(x, 1), :], (16, 16))
        column = jnp.sum(jnp.where(eye, line, 0.0), axis=1, keepdims=True)
        field[DR, x + 2, pl.ds(2, 16), :] = jnp.where(
            on_plane, jnp.broadcast_to(column, (16, 128)), 0.0
        )

    loop(0, 16, 4, make_drive)

    loads[2].wait()

    def make_coef(p):
        field[CO, p, pl.ds(2, 16), :] = courant / field[CO, p, pl.ds(2, 16), :]

    loop(2, 16, 4, make_coef)

    start_aux()

    total_x = n_x * 16
    total_y = n_y * 16

    def profile(cells, total, width):
        place = cells.astype(F32)
        dist = jnp.minimum(place, total - 1.0 - place)
        wide = jnp.full(cells.shape, width, jnp.int32).astype(F32)
        return jnp.maximum(0.0, (wide - dist) / wide) ** 2

    loads[5].wait()
    ys = gy * 16 - 2 + lax.broadcasted_iota(jnp.int32, (ROWS, 128), 0)
    prof_y = profile(ys, total_y, pml_ref[1])
    in_y = (ys >= 0) & (ys < total_y)

    def make_damp(p):
        xs = jnp.full((ROWS, 128), gx * 16 - 2 + p, jnp.int32)
        value = jnp.exp(-absorb * (profile(xs, total_x, pml_ref[0]) + prof_y))
        keep = in_y & (xs >= 0) & (xs < total_x)
        damp[p] = jnp.where(keep, value, 0.0)

    loop(0, 20, 4, make_damp)

    loads[6].wait()
    row_id = lax.broadcasted_iota(jnp.int32, (8, 128), 0)
    tval = (row_id % 2 + 1).astype(F32)
    omega = jnp.where(
        row_id < 2, jnp.full((8, 128), freq_ref[0, 0]), jnp.full((8, 128), freq_ref[0, 1])
    )
    trig[0:8] = jnp.cos(omega * tval)
    trig[8:16] = jnp.sin(omega * tval)

    loads[8].wait()
    loads[3].wait()
    loads[4].wait()

    blocks = blocks_ref[...]
    masks = []
    for bx in range(2):
        for by in range(2):
            cell = (gx * 2 + bx) * (total_y // BS) + gy * 2 + by
            hit = jnp.where(blocks == cell, 1.0, 0.0)
            masks.append(jnp.max(hit, axis=1, keepdims=True))
    upper = lax.broadcasted_iota(jnp.int32, (16, 128), 0) < 8

    def make_weights(bx):
        mask = jnp.where(
            upper,
            jnp.broadcast_to(masks[2 * bx], (16, 128)),
            jnp.broadcast_to(masks[2 * bx + 1], (16, 128)),
        )

        def step(x):
            for k in range(2):
                c1 = trig[pl.ds(2 * k, 1), :]
                c2 = trig[pl.ds(2 * k + 1, 1), :]
                s1 = trig[pl.ds(8 + 2 * k, 1), :]
                s2 = trig[pl.ds(8 + 2 * k + 1, 1), :]
                first = None
                for c in range(3):
                    fr = fwd[k, 0, c, x].astype(F32) * mask
                    fi = fwd[k, 1, c, x].astype(F32) * mask
                    ar = adj[k, 0, c, x].astype(F32)
                    ai = adj[k, 1, c, x].astype(F32)
                    part = fr * ar + fi * ai
                    first = part if first is None else first + part
                    weights[x, k * 7 + 1 + c, pl.ds(2, 16), :] = fr * c1 - fi * s1
                    weights[x, k * 7 + 4 + c, pl.ds(2, 16), :] = fr * c2 - fi * s2
                weights[x, k * 7, pl.ds(2, 16), :] = first

        loop(bx * 8, 8, 1, step)

    make_weights(0)
    make_weights(1)

    loads[0].wait()
    loads[1].wait()

    for dx, dy in order:

        @pl.when(inside(-dx, -dy))
        def _(dx=dx, dy=dy):
            for copy in halo(dx, dy):
                copy.wait_recv()
            if (dx, dy) in aux_order:
                aux(dx, dy).wait_recv()

    lane = lax.broadcasted_iota(jnp.int32, (ROWS, 128), 1)
    not_last = lane < 127
    not_first = lane > 0

    def ahead_z(v):
        return jnp.where(not_last, pltpu.roll(v, 127, 1), 0.0) - v

    def behind_z(v):
        return v - jnp.where(not_first, pltpu.roll(v, 1, 1), 0.0)

    def ahead_y(v):
        return pltpu.roll(v, ROWS - 1, 0) - v

    def behind_y(v):
        return v - pltpu.roll(v, 1, 0)

    def magnetic(p, e, ahead, h):
        d = damp[p]
        ex, ey, ez = e
        hx = d * (h[0] - courant * (ahead_y(ez) - ahead_z(ey)))
        hy = d * (h[1] - courant * (ahead_z(ex) - (ahead[2] - ez)))
        hz = d * (h[2] - courant * ((ahead[1] - ey) - ahead_y(ex)))
        return hx, hy, hz

    def electric(p, h, behind, e, sine):
        d = damp[p]
        co = field[CO, p]
        hx, hy, hz = h
        ex = d * (e[0] + co * (behind_y(hz) - behind_z(hy)))
        ey = d * (e[1] + co * (behind_z(hx) - (hz - behind[2])))
        ez = d * (e[2] + co * ((hy - behind[1]) - behind_y(hx)) + field[DR, p] * sine)
        return ex, ey, ez

    sine1 = trig[pl.ds(8, 1), :]
    sine2 = trig[pl.ds(9, 1), :]

    def read(first, p):
        return tuple(field[first + c, p] for c in range(3))

    lane_x = grp % 4
    others = [(1, 2), (1, 1), (1, 3), (1, 0), (0, 2), (0, 1), (0, 3)]

    def peer(dz, dx):
        return (z_hi + dz) % 2, (lane_x + dx) % 4

    def send_quarter(q):
        for dz, dx in others:
            k, j = peer(dz, dx)
            pltpu.make_async_remote_copy(
                src_ref=term.at[k, 4 * q + j, pl.ds(2, 16), :],
                dst_ref=landed.at[grp, q],
                send_sem=red_send,
                recv_sem=red_recv,
                device_id={"grp": k * 4 + j},
                device_id_type=MESH,
            ).start()

    e0 = read(EX, 0)
    h1 = e1 = h2 = None
    for p in range(19):
        e0_next = read(EX, p + 1)
        h1_last, e1_last, h2_last = h1, e1, h2
        h1 = magnetic(p, e0, e0_next, read(HX, p))
        if p >= 1:
            e1 = electric(p, h1, h1_last, e0, sine1)
        if p >= 2:
            h2 = magnetic(p - 1, e1_last, e1, h1_last)
        if p >= 3:
            e2 = electric(p - 1, h2, h2_last, e1_last, sine2)
            x = p - 3
            for k in range(2):
                value = weights[x, k * 7]
                for c in range(3):
                    value = value + weights[x, k * 7 + 1 + c] * e1_last[c]
                    value = value + weights[x, k * 7 + 4 + c] * e2[c]
                term[k, x] = value
            if x % 4 == 3:
                send_quarter(x // 4)
        e0 = e0_next

    for q in range(4):
        landed[grp, q] = term[z_hi, 4 * q + lane_x, 2:18, :]
    seven = landed.at[pl.ds(0, 7)]
    pltpu.make_async_copy(seven, seven, red_recv).wait()

    total = landed[0]
    for j in range(1, 8):
        total = total + landed[j]
    summed[z_hi, :, lane_x] = total
    square = jnp.sum(total * total, axis=0)
    line = jnp.sum(square, axis=0, keepdims=True)

    me1 = lane_x * 8 + gy
    me2 = z_hi * 8 + gx
    row1[...] = line
    rows1[pl.ds(me1, 1), :] = line
    steps = [(dx, dy) for dx in range(4) for dy in range(8) if (dx, dy) != (0, 0)]
    for dx, dy in sorted(steps, key=lambda d: -min(d[0], 4 - d[0]) - min(d[1], 8 - d[1])):
        pltpu.make_async_remote_copy(
            src_ref=row1,
            dst_ref=rows1.at[pl.ds(me1, 1)],
            send_sem=s1_send,
            recv_sem=s1_recv,
            device_id={"grp": z_hi * 4 + (lane_x + dx) % 4, "gy": (gy + dy) % 8},
            device_id_type=MESH,
        ).start()

    mine = summed.at[z_hi, :, lane_x]
    for dz, dx in others:
        k, j = peer(dz, dx)
        pltpu.make_async_remote_copy(
            src_ref=mine,
            dst_ref=mine,
            send_sem=gat_send,
            recv_sem=gat_recv,
            device_id={"grp": k * 4 + j},
            device_id_type=MESH,
        ).start()

    some = rows1.at[pl.ds(0, 31)]
    pltpu.make_async_copy(some, some, s1_recv).wait()
    line = jnp.sum(rows1[...], axis=0, keepdims=True)
    row2[...] = line
    rows2[pl.ds(me2, 1), :] = line
    place = me2 // 2
    steps = [(dz, dc) for dz in range(8) for dc in range(2) if (dz, dc) != (0, 0)]
    for dz, dc in sorted(steps, key=lambda d: -min(d[0], 8 - d[0])):
        to_z = (place + dz) % 8
        pltpu.make_async_remote_copy(
            src_ref=row2,
            dst_ref=rows2.at[pl.ds(me2, 1)],
            send_sem=s2_send,
            recv_sem=s2_recv,
            device_id={
                "grp": (to_z // 4) * 4 + lane_x,
                "gx": (to_z % 4) * 2 + (gx + dc) % 2,
            },
            device_id_type=MESH,
        ).start()

    pltpu.make_async_copy(seven, seven, gat_recv).wait()
    out = pltpu.make_async_copy(summed, grad_hbm, out_sem)
    out.start()

    few = rows2.at[pl.ds(0, 15)]
    pltpu.make_async_copy(few, few, s2_recv).wait()
    count = float(128 * BS * BS * 128)
    for k in range(2):
        squares = jnp.sum(rows2[8 * k : 8 * k + 8], axis=0, keepdims=True)
        squares = jnp.sum(squares, axis=1, keepdims=True)
        value = lax.rsqrt(squares / count + 1e-05)
        scale_ref[k] = jnp.broadcast_to(value, (8, 128))

    out.wait()
    pltpu.make_async_copy(seven, seven, red_send).wait()
    pltpu.make_async_copy(seven, seven, gat_send).wait()
    pltpu.make_async_copy(some, some, s1_send).wait()
    pltpu.make_async_copy(few, few, s2_send).wait()
    for dx, dy in order:

        @pl.when(inside(dx, dy))
        def _(dx=dx, dy=dy):
            for copy in halo(dx, dy):
                copy.wait_send()
            if (dx, dy) in aux_order:
                aux(dx, dy).wait_send()


def body(
    efield,
    hfield,
    fwd_dft,
    adj_dft,
    permittivity,
    source_amp,
    source_plane,
    freqs,
    pml_width,
    design_blocks,
):
    hbm = pl.BlockSpec(memory_space=pltpu.HBM)
    def pin(value):
        return pltpu.with_memory_space_constraint(value, pltpu.HBM)

    vmem = pl.BlockSpec(memory_space=pltpu.VMEM)
    dma = pltpu.SemaphoreType.DMA
    grad, scale = pl.pallas_call(
        kernel,
        out_shape=(
            jax.ShapeDtypeStruct((2, 4, 4, 16, 128), F32),
            jax.ShapeDtypeStruct((2, 8, 128), F32),
        ),
        in_specs=[hbm] * 6 + [pl.BlockSpec(memory_space=pltpu.SMEM)] + [hbm] * 3,
        out_specs=(pl.BlockSpec(memory_space=pl.ANY), vmem),
        scratch_shapes=[
            pltpu.VMEM((8, PLANES, ROWS, 128), F32),
            pltpu.VMEM((20, ROWS, 128), F32),
            pltpu.VMEM((2, 2, 3, 16, 16, 128), jnp.bfloat16),
            pltpu.VMEM((2, 2, 3, 16, 16, 128), jnp.bfloat16),
            pltpu.VMEM((16, 128), F32),
            pltpu.VMEM((16, 14, ROWS, 128), F32),
            pltpu.VMEM((2, 16, ROWS, 128), F32),
            pltpu.VMEM((8, 4, 16, 128), F32),
            pltpu.VMEM((2, 4, 4, 16, 128), F32),
            pltpu.VMEM((1, 128), F32),
            pltpu.VMEM((32, 128), F32),
            pltpu.VMEM((1, 128), F32),
            pltpu.VMEM((16, 128), F32),
            pltpu.VMEM((1, 16, 16), F32),
            pltpu.SMEM((1, 2), F32),
            pltpu.SMEM((2,), jnp.int32),
            pltpu.VMEM((1, 128), jnp.int32),
            dma((9,)),
            dma((32,)),
            dma((32,)),
            dma,
            dma,
            dma,
            dma,
            dma,
            dma,
            dma,
            dma,
            dma,
        ],
        compiler_params=pltpu.CompilerParams(
            collective_id=0, has_side_effects=True, vmem_limit_bytes=40 * 1024 * 1024
        ),
        name="adjoint",
    )(
        *map(pin, (efield, hfield, fwd_dft, adj_dft, permittivity, source_amp)),
        source_plane,
        *map(pin, (freqs, pml_width, design_blocks[None, :])),
    )
    return grad.reshape(2, 16, 16, 128) * scale[:, :1, None, :]


def solution(mesh):
    in_specs = (
        P("grp", None, "gx", "gy", None),
        P("grp", None, "gx", "gy", None),
        P("grp", None, None, None, "gx", "gy", None),
        P("grp", None, None, None, "gx", "gy", None),
        P("gx", "gy", None),
        P("grp", "gx", "gy"),
        P("grp"),
        P("grp", None),
        P(),
        P(),
    )
    out_specs = P(None, "gx", "gy", None)
    return jax.shard_map(body, mesh=mesh, in_specs=in_specs, out_specs=out_specs, check_vma=False)
```

```python
import functools

import jax
import jax.numpy as jnp
from jax import lax
from jax.experimental import pallas as pl
from jax.experimental.pallas import tpu as pltpu
from jax.sharding import PartitionSpec as P

BS = 8
MESH = pl.DeviceIdType.MESH
F32 = jnp.float32

courant = 0.5
absorb = 0.8

PLANES = 21
ROWS = 24
EX, EY, EZ, HX, HY, HZ, CO, DR = range(8)


def loop(low, count, unroll, step):
    assert count % unroll == 0

    def body(i, carry):
        for u in range(unroll):
            step(low + i * unroll + u)
        return carry

    lax.fori_loop(0, count // unroll, body, 0)


def kernel(
    e_hbm,
    h_hbm,
    fwd_hbm,
    adj_hbm,
    perm_hbm,
    amp_hbm,
    plane_ref,
    freq_hbm,
    pml_hbm,
    blocks_hbm,
    grad_hbm,
    scale_ref,
    field,
    damp,
    fwd,
    adj,
    trig,
    weights,
    term,
    landed,
    summed,
    row1,
    rows1,
    row2,
    rows2,
    amp_ref,
    freq_ref,
    pml_ref,
    blocks_ref,
    load_sem,
    halo_send,
    halo_recv,
    red_send,
    red_recv,
    gat_send,
    gat_recv,
    s1_send,
    s1_recv,
    s2_send,
    s2_recv,
    out_sem,
    round1,
    round2,
):
    grp = lax.axis_index("grp")
    gx = lax.axis_index("gx")
    gy = lax.axis_index("gy")
    z_hi = grp // 4
    n_x = 8
    n_y = 8

    lane_x = grp % 4
    z_lo = gx // 2
    core = gx % 2
    place = z_hi * 4 + z_lo
    sides = [(dx, dy) for dx in (-1, 0, 1) for dy in (-1, 0, 1) if (dx, dy) != (0, 0)]

    def device(x=0, y=0, z=0, c=0):
        there = (place + z) % 8
        return {
            "grp": (there // 4) * 4 + (lane_x + x) % 4,
            "gx": (there % 4) * 2 + (core + c) % 2,
            "gy": (gy + y) % 8,
        }

    def tell(semaphore, **steps):
        pl.semaphore_signal(
            semaphore, inc=1, device_id=device(**steps), device_id_type=MESH
        )

    barrier = pltpu.get_barrier_semaphore()
    beyond = 2 * core - 1
    for y in (-1, 1, 0):
        tell(barrier, y=y, z=beyond, c=1)
    for y in (-1, 1, 0):
        tell(barrier, y=y, c=1)
    for y in (-1, 1, -2, 2):
        tell(barrier, y=y)

    own = (pl.ds(2, 16), pl.ds(2, 16))
    loads = [
        pltpu.make_async_copy(e_hbm.at[0], field.at[(pl.ds(EX, 3), *own)], load_sem.at[0]),
        pltpu.make_async_copy(h_hbm.at[0], field.at[(pl.ds(HX, 3), *own)], load_sem.at[1]),
        pltpu.make_async_copy(perm_hbm, field.at[(CO, *own)], load_sem.at[2]),
        pltpu.make_async_copy(fwd_hbm.at[0], fwd, load_sem.at[3]),
        pltpu.make_async_copy(adj_hbm.at[0], adj, load_sem.at[4]),
        pltpu.make_async_copy(pml_hbm, pml_ref, load_sem.at[5]),
        pltpu.make_async_copy(freq_hbm, freq_ref, load_sem.at[6]),
        pltpu.make_async_copy(amp_hbm, amp_ref, load_sem.at[7]),
        pltpu.make_async_copy(blocks_hbm, blocks_ref, load_sem.at[8]),
    ]
    for i in (5, 2, 7, 0, 1, 6, 3, 4, 8):
        loads[i].start()

    for z in (-2, 2, -1, 1):
        tell(barrier, z=z)
    for x in (2, 1, 3):
        tell(barrier, x=x)

    def inside(dx, dy):
        ok = None
        for d, me, n in ((dx, gx, n_x), (dy, gy, n_y)):
            if d != 0:
                here = (me > 0) if d < 0 else (me < n - 1)
                ok = here if ok is None else jnp.logical_and(ok, here)
        return ok

    pl.semaphore_wait(barrier, 17)
    for step in (-2, 2):
        tell(round1, z=step)
        tell(round1, y=step)

    def pick(d, wide):
        if d == 0:
            return pl.ds(0, 16), pl.ds(2, 16)
        if d > 0:
            return pl.ds(16 - wide, wide), pl.ds(2 - wide, wide)
        return pl.ds(0, wide), pl.ds(18, wide)

    e_arg, h_arg = e_hbm.at[0], h_hbm.at[0]
    parts = {
        (1, 0): [(e_arg, EX, 0, 3, 2, 0), (h_arg, HX, 1, 2, 2, 0), (h_arg, HX, 0, 1, 1, 0)],
        (-1, 0): [(e_arg, EX, 1, 2, 2, 0), (h_arg, HX, 0, 3, 1, 0), (e_arg, EX, 0, 1, 1, 0)],
        (0, 1): [(e_arg, EX, 0, 3, 0, 2), (h_arg, HX, 0, 3, 0, 2)],
        (0, -1): [(e_arg, EX, 0, 3, 0, 2), (h_arg, HX, 0, 3, 0, 1)],
        (1, 1): [(e_arg, EX, 0, 3, 1, 1), (h_arg, HX, 0, 3, 1, 1)],
        (1, -1): [(e_arg, EX, 0, 3, 2, 2), (h_arg, HX, 0, 3, 1, 1)],
        (-1, 1): [(e_arg, EX, 0, 3, 2, 2), (h_arg, HX, 0, 3, 1, 1)],
        (-1, -1): [(e_arg, EX, 0, 3, 1, 1)],
    }

    def halo(dx, dy):
        copies = []
        for i, (source, base, first, many, wide_x, wide_y) in enumerate(parts[dx, dy]):
            from_x, to_x = pick(dx, wide_x)
            from_y, to_y = pick(dy, wide_y)
            slot = 3 * sides.index((dx, dy)) + i
            copies.append(
                pltpu.make_async_remote_copy(
                    src_ref=source.at[pl.ds(first, many), from_x, from_y, :],
                    dst_ref=field.at[pl.ds(base + first, many), to_x, to_y, :],
                    send_sem=halo_send.at[slot],
                    recv_sem=halo_recv.at[slot],
                    device_id={"gx": gx + dx, "gy": gy + dy},
                    device_id_type=MESH,
                )
            )
        return copies

    def aux(dx, dy):
        from_x, to_x = pick(dx, 1)
        from_y, to_y = pick(dy, 1)
        slot = 24 + sides.index((dx, dy))
        inner_x = pl.ds(from_x.start + 2, from_x.size)
        inner_y = pl.ds(from_y.start + 2, from_y.size)
        return pltpu.make_async_remote_copy(
            src_ref=field.at[pl.ds(CO, 2), inner_x, inner_y, :],
            dst_ref=field.at[pl.ds(CO, 2), to_x, to_y, :],
            send_sem=halo_send.at[slot],
            recv_sem=halo_recv.at[slot],
            device_id={"gx": gx + dx, "gy": gy + dy},
            device_id_type=MESH,
        )

    order = [(0, 1), (0, -1), (1, 0), (-1, 0), (1, -1), (-1, 1), (1, 1), (-1, -1)]
    aux_order = [side for side in order if side not in ((1, 1), (-1, -1))]

    for dx, dy in order:

        @pl.when(inside(dx, dy))
        def _(dx=dx, dy=dy):
            for copy in halo(dx, dy):
                copy.start()

    def start_aux():
        for dx, dy in aux_order:

            @pl.when(inside(dx, dy))
            def _(dx=dx, dy=dy):
                aux(dx, dy).start()

    @pl.when(gx == 0)
    def _():
        field[:, 0:2] = jnp.zeros((8, 2, ROWS, 128), F32)

    @pl.when(gx == n_x - 1)
    def _():
        field[:, 18:20] = jnp.zeros((8, 2, ROWS, 128), F32)

    @pl.when(gy == 0)
    def _():
        field[:, 0:20, 0:2, :] = jnp.zeros((8, 20, 2, 128), F32)

    @pl.when(gy == n_y - 1)
    def _():
        field[:, 0:20, 18:20, :] = jnp.zeros((8, 20, 2, 128), F32)

    eye = lax.broadcasted_iota(jnp.int32, (16, 16), 0) == lax.broadcasted_iota(
        jnp.int32, (16, 16), 1
    )
    loads[7].wait()
    lane16 = lax.broadcasted_iota(jnp.int32, (16, 128), 1)
    on_plane = lane16 == plane_ref[0]

    def make_drive(x):
        line = jnp.broadcast_to(amp_ref[0, pl.ds(x, 1), :], (16, 16))
        column = jnp.sum(jnp.where(eye, line, 0.0), axis=1, keepdims=True)
        field[DR, x + 2, pl.ds(2, 16), :] = jnp.where(
            on_plane, jnp.broadcast_to(column, (16, 128)), 0.0
        )

    loop(0, 16, 4, make_drive)

    loads[2].wait()

    def make_coef(p):
        field[CO, p, pl.ds(2, 16), :] = courant / field[CO, p, pl.ds(2, 16), :]

    loop(2, 16, 4, make_coef)

    start_aux()

    total_x = n_x * 16
    total_y = n_y * 16

    def profile(cells, total, width):
        place = cells.astype(F32)
        dist = jnp.minimum(place, total - 1.0 - place)
        wide = jnp.full(cells.shape, width, jnp.int32).astype(F32)
        return jnp.maximum(0.0, (wide - dist) / wide) ** 2

    loads[5].wait()
    ys = gy * 16 - 2 + lax.broadcasted_iota(jnp.int32, (ROWS, 128), 0)
    prof_y = profile(ys, total_y, pml_ref[1])
    in_y = (ys >= 0) & (ys < total_y)

    def make_damp(p):
        xs = jnp.full((ROWS, 128), gx * 16 - 2 + p, jnp.int32)
        value = jnp.exp(-absorb * (profile(xs, total_x, pml_ref[0]) + prof_y))
        keep = in_y & (xs >= 0) & (xs < total_x)
        damp[p] = jnp.where(keep, value, 0.0)

    loop(0, 20, 4, make_damp)

    pl.semaphore_wait(round1, 4)
    for x in (2, 1, 3):
        tell(round2, x=x)
    tell(round2, c=1)

    loads[6].wait()
    row_id = lax.broadcasted_iota(jnp.int32, (8, 128), 0)
    tval = (row_id % 2 + 1).astype(F32)
    omega = jnp.where(
        row_id < 2, jnp.full((8, 128), freq_ref[0, 0]), jnp.full((8, 128), freq_ref[0, 1])
    )
    trig[0:8] = jnp.cos(omega * tval)
    trig[8:16] = jnp.sin(omega * tval)

    loads[8].wait()
    loads[3].wait()
    loads[4].wait()

    blocks = blocks_ref[...]
    masks = []
    for bx in range(2):
        for by in range(2):
            cell = (gx * 2 + bx) * (total_y // BS) + gy * 2 + by
            hit = jnp.where(blocks == cell, 1.0, 0.0)
            masks.append(jnp.max(hit, axis=1, keepdims=True))
    upper = lax.broadcasted_iota(jnp.int32, (16, 128), 0) < 8

    def make_weights(bx):
        mask = jnp.where(
            upper,
            jnp.broadcast_to(masks[2 * bx], (16, 128)),
            jnp.broadcast_to(masks[2 * bx + 1], (16, 128)),
        )

        def step(x):
            for k in range(2):
                c1 = trig[pl.ds(2 * k, 1), :]
                c2 = trig[pl.ds(2 * k + 1, 1), :]
                s1 = trig[pl.ds(8 + 2 * k, 1), :]
                s2 = trig[pl.ds(8 + 2 * k + 1, 1), :]
                first = None
                for c in range(3):
                    fr = fwd[k, 0, c, x].astype(F32) * mask
                    fi = fwd[k, 1, c, x].astype(F32) * mask
                    ar = adj[k, 0, c, x].astype(F32)
                    ai = adj[k, 1, c, x].astype(F32)
                    part = fr * ar + fi * ai
                    first = part if first is None else first + part
                    weights[x, k * 7 + 1 + c, pl.ds(2, 16), :] = fr * c1 - fi * s1
                    weights[x, k * 7 + 4 + c, pl.ds(2, 16), :] = fr * c2 - fi * s2
                weights[x, k * 7, pl.ds(2, 16), :] = first

        loop(bx * 8, 8, 1, step)

    make_weights(0)
    make_weights(1)

    pl.semaphore_wait(round2, 4)
    loads[0].wait()
    loads[1].wait()

    for dx, dy in order:

        @pl.when(inside(-dx, -dy))
        def _(dx=dx, dy=dy):
            for copy in halo(dx, dy):
                copy.wait_recv()
            if (dx, dy) in aux_order:
                aux(dx, dy).wait_recv()

    lane = lax.broadcasted_iota(jnp.int32, (ROWS, 128), 1)
    not_last = lane < 127
    not_first = lane > 0

    def ahead_z(v):
        return jnp.where(not_last, pltpu.roll(v, 127, 1), 0.0) - v

    def behind_z(v):
        return v - jnp.where(not_first, pltpu.roll(v, 1, 1), 0.0)

    def ahead_y(v):
        return pltpu.roll(v, ROWS - 1, 0) - v

    def behind_y(v):
        return v - pltpu.roll(v, 1, 0)

    def magnetic(p, e, ahead, h):
        d = damp[p]
        ex, ey, ez = e
        hx = d * (h[0] - courant * (ahead_y(ez) - ahead_z(ey)))
        hy = d * (h[1] - courant * (ahead_z(ex) - (ahead[2] - ez)))
        hz = d * (h[2] - courant * ((ahead[1] - ey) - ahead_y(ex)))
        return hx, hy, hz

    def electric(p, h, behind, e, sine):
        d = damp[p]
        co = field[CO, p]
        hx, hy, hz = h
        ex = d * (e[0] + co * (behind_y(hz) - behind_z(hy)))
        ey = d * (e[1] + co * (behind_z(hx) - (hz - behind[2])))
        ez = d * (e[2] + co * ((hy - behind[1]) - behind_y(hx)) + field[DR, p] * sine)
        return ex, ey, ez

    sine1 = trig[pl.ds(8, 1), :]
    sine2 = trig[pl.ds(9, 1), :]

    def read(first, p):
        return tuple(field[first + c, p] for c in range(3))

    others = [(1, 2), (1, 1), (1, 3), (1, 0), (0, 2), (0, 1), (0, 3)]

    def peer(dz, dx):
        return (z_hi + dz) % 2, (lane_x + dx) % 4

    def send_quarter(q):
        for dz, dx in others:
            k, j = peer(dz, dx)
            pltpu.make_async_remote_copy(
                src_ref=term.at[k, 4 * q + j, pl.ds(2, 16), :],
                dst_ref=landed.at[grp, q],
                send_sem=red_send,
                recv_sem=red_recv,
                device_id={"grp": k * 4 + j},
                device_id_type=MESH,
            ).start()

    e0 = read(EX, 0)
    h1 = e1 = h2 = None
    for p in range(19):
        e0_next = read(EX, p + 1)
        h1_last, e1_last, h2_last = h1, e1, h2
        h1 = magnetic(p, e0, e0_next, read(HX, p))
        if p >= 1:
            e1 = electric(p, h1, h1_last, e0, sine1)
        if p >= 2:
            h2 = magnetic(p - 1, e1_last, e1, h1_last)
        if p >= 3:
            e2 = electric(p - 1, h2, h2_last, e1_last, sine2)
            x = p - 3
            for k in range(2):
                value = weights[x, k * 7]
                for c in range(3):
                    value = value + weights[x, k * 7 + 1 + c] * e1_last[c]
                    value = value + weights[x, k * 7 + 4 + c] * e2[c]
                term[k, x] = value
            if x % 4 == 3:
                send_quarter(x // 4)
        e0 = e0_next

    for q in range(4):
        landed[grp, q] = term[z_hi, 4 * q + lane_x, 2:18, :]
    seven = landed.at[pl.ds(0, 7)]
    pltpu.make_async_copy(seven, seven, red_recv).wait()

    total = landed[0]
    for j in range(1, 8):
        total = total + landed[j]
    summed[z_hi, :, lane_x] = total
    square = jnp.sum(total * total, axis=0)
    line = jnp.sum(square, axis=0, keepdims=True)

    me1 = lane_x * 8 + gy
    me2 = z_hi * 8 + gx
    row1[...] = line
    rows1[pl.ds(me1, 1), :] = line
    steps = [(dx, dy) for dx in range(4) for dy in range(8) if (dx, dy) != (0, 0)]
    for dx, dy in sorted(steps, key=lambda d: -min(d[0], 4 - d[0]) - min(d[1], 8 - d[1])):
        pltpu.make_async_remote_copy(
            src_ref=row1,
            dst_ref=rows1.at[pl.ds(me1, 1)],
            send_sem=s1_send,
            recv_sem=s1_recv,
            device_id={"grp": z_hi * 4 + (lane_x + dx) % 4, "gy": (gy + dy) % 8},
            device_id_type=MESH,
        ).start()

    mine = summed.at[z_hi, :, lane_x]
    for dz, dx in others:
        k, j = peer(dz, dx)
        pltpu.make_async_remote_copy(
            src_ref=mine,
            dst_ref=mine,
            send_sem=gat_send,
            recv_sem=gat_recv,
            device_id={"grp": k * 4 + j},
            device_id_type=MESH,
        ).start()

    some = rows1.at[pl.ds(0, 31)]
    pltpu.make_async_copy(some, some, s1_recv).wait()
    line = jnp.sum(rows1[...], axis=0, keepdims=True)
    row2[...] = line
    rows2[pl.ds(me2, 1), :] = line
    steps = [(dz, dc) for dz in range(8) for dc in range(2) if (dz, dc) != (0, 0)]
    for dz, dc in sorted(steps, key=lambda d: -min(d[0], 8 - d[0])):
        to_z = (place + dz) % 8
        pltpu.make_async_remote_copy(
            src_ref=row2,
            dst_ref=rows2.at[pl.ds(me2, 1)],
            send_sem=s2_send,
            recv_sem=s2_recv,
            device_id={
                "grp": (to_z // 4) * 4 + lane_x,
                "gx": (to_z % 4) * 2 + (gx + dc) % 2,
            },
            device_id_type=MESH,
        ).start()

    pltpu.make_async_copy(seven, seven, gat_recv).wait()
    out = pltpu.make_async_copy(summed, grad_hbm, out_sem)
    out.start()

    few = rows2.at[pl.ds(0, 15)]
    pltpu.make_async_copy(few, few, s2_recv).wait()
    count = float(128 * BS * BS * 128)
    for k in range(2):
        squares = jnp.sum(rows2[8 * k : 8 * k + 8], axis=0, keepdims=True)
        squares = jnp.sum(squares, axis=1, keepdims=True)
        value = lax.rsqrt(squares / count + 1e-05)
        scale_ref[k] = jnp.broadcast_to(value, (8, 128))

    out.wait()
    pltpu.make_async_copy(seven, seven, red_send).wait()
    pltpu.make_async_copy(seven, seven, gat_send).wait()
    pltpu.make_async_copy(some, some, s1_send).wait()
    pltpu.make_async_copy(few, few, s2_send).wait()
    for dx, dy in order:

        @pl.when(inside(dx, dy))
        def _(dx=dx, dy=dy):
            for copy in halo(dx, dy):
                copy.wait_send()
            if (dx, dy) in aux_order:
                aux(dx, dy).wait_send()


def body(
    efield,
    hfield,
    fwd_dft,
    adj_dft,
    permittivity,
    source_amp,
    source_plane,
    freqs,
    pml_width,
    design_blocks,
):
    hbm = pl.BlockSpec(memory_space=pltpu.HBM)
    def pin(value):
        return pltpu.with_memory_space_constraint(value, pltpu.HBM)

    vmem = pl.BlockSpec(memory_space=pltpu.VMEM)
    dma = pltpu.SemaphoreType.DMA
    grad, scale = pl.pallas_call(
        kernel,
        out_shape=(
            jax.ShapeDtypeStruct((2, 4, 4, 16, 128), F32),
            jax.ShapeDtypeStruct((2, 8, 128), F32),
        ),
        in_specs=[hbm] * 6 + [pl.BlockSpec(memory_space=pltpu.SMEM)] + [hbm] * 3,
        out_specs=(pl.BlockSpec(memory_space=pl.ANY), vmem),
        scratch_shapes=[
            pltpu.VMEM((8, PLANES, ROWS, 128), F32),
            pltpu.VMEM((20, ROWS, 128), F32),
            pltpu.VMEM((2, 2, 3, 16, 16, 128), jnp.bfloat16),
            pltpu.VMEM((2, 2, 3, 16, 16, 128), jnp.bfloat16),
            pltpu.VMEM((16, 128), F32),
            pltpu.VMEM((16, 14, ROWS, 128), F32),
            pltpu.VMEM((2, 16, ROWS, 128), F32),
            pltpu.VMEM((8, 4, 16, 128), F32),
            pltpu.VMEM((2, 4, 4, 16, 128), F32),
            pltpu.VMEM((1, 128), F32),
            pltpu.VMEM((32, 128), F32),
            pltpu.VMEM((1, 128), F32),
            pltpu.VMEM((16, 128), F32),
            pltpu.VMEM((1, 16, 16), F32),
            pltpu.SMEM((1, 2), F32),
            pltpu.SMEM((2,), jnp.int32),
            pltpu.VMEM((1, 128), jnp.int32),
            dma((9,)),
            dma((32,)),
            dma((32,)),
            dma,
            dma,
            dma,
            dma,
            dma,
            dma,
            dma,
            dma,
            dma,
            pltpu.SemaphoreType.REGULAR,
            pltpu.SemaphoreType.REGULAR,
        ],
        compiler_params=pltpu.CompilerParams(
            collective_id=0, has_side_effects=True, vmem_limit_bytes=40 * 1024 * 1024
        ),
        name="adjoint",
    )(
        *map(pin, (efield, hfield, fwd_dft, adj_dft, permittivity, source_amp)),
        source_plane,
        *map(pin, (freqs, pml_width, design_blocks[None, :])),
    )
    return grad.reshape(2, 16, 16, 128) * scale[:, :1, None, :]


def solution(mesh):
    in_specs = (
        P("grp", None, "gx", "gy", None),
        P("grp", None, "gx", "gy", None),
        P("grp", None, None, None, "gx", "gy", None),
        P("grp", None, None, None, "gx", "gy", None),
        P("gx", "gy", None),
        P("grp", "gx", "gy"),
        P("grp"),
        P("grp", None),
        P(),
        P(),
    )
    out_specs = P(None, "gx", "gy", None)
    return jax.shard_map(body, mesh=mesh, in_specs=in_specs, out_specs=out_specs, check_vma=False)
```

```python
import functools

import jax
import jax.numpy as jnp
from jax import lax
from jax.experimental import pallas as pl
from jax.experimental.pallas import tpu as pltpu
from jax.sharding import PartitionSpec as P

BS = 8
MESH = pl.DeviceIdType.MESH
F32 = jnp.float32

courant = 0.5
absorb = 0.8

PLANES = 21
ROWS = 24
READY = (7, 15)
EX, EY, EZ, HX, HY, HZ, CO, DR = range(8)


def loop(low, count, unroll, step):
    assert count % unroll == 0

    def body(i, carry):
        for u in range(unroll):
            step(low + i * unroll + u)
        return carry

    lax.fori_loop(0, count // unroll, body, 0)


def kernel(
    e_hbm,
    h_hbm,
    fwd_hbm,
    adj_hbm,
    perm_hbm,
    amp_hbm,
    plane_ref,
    freq_hbm,
    pml_hbm,
    blocks_hbm,
    grad_out,
    scale_ref,
    field,
    damp,
    fwd,
    adj,
    trig,
    weights,
    term,
    landed,
    summed,
    row1,
    rows1,
    row2,
    rows2,
    amp_ref,
    freq_ref,
    pml_ref,
    blocks_ref,
    load_sem,
    halo_send,
    halo_recv,
    red_send,
    red_recv,
    gat_send,
    gat_recv,
    s1_send,
    s1_recv,
    s2_send,
    s2_recv,
    out_sem,
    round1,
    round2,
):
    grp = lax.axis_index("grp")
    gx = lax.axis_index("gx")
    gy = lax.axis_index("gy")
    z_hi = grp // 4
    n_x = 8
    n_y = 8

    lane_x = grp % 4
    z_lo = gx // 2
    core = gx % 2
    place = z_hi * 4 + z_lo
    sides = [(dx, dy) for dx in (-1, 0, 1) for dy in (-1, 0, 1) if (dx, dy) != (0, 0)]

    def device(x=0, y=0, z=0, c=0):
        there = (place + z) % 8
        return {
            "grp": (there // 4) * 4 + (lane_x + x) % 4,
            "gx": (there % 4) * 2 + (core + c) % 2,
            "gy": (gy + y) % 8,
        }

    def tell(semaphore, **steps):
        pl.semaphore_signal(
            semaphore, inc=1, device_id=device(**steps), device_id_type=MESH
        )

    barrier = pltpu.get_barrier_semaphore()
    beyond = 2 * core - 1
    for y in (-1, 1, 0):
        tell(barrier, y=y, z=beyond, c=1)
    for y in (-1, 1, 0):
        tell(barrier, y=y, c=1)
    for y in (-1, 1, -2, 2):
        tell(barrier, y=y)

    own = (pl.ds(2, 16), pl.ds(2, 16))
    loads = [
        pltpu.make_async_copy(e_hbm.at[0], field.at[(pl.ds(EX, 3), *own)], load_sem.at[0]),
        pltpu.make_async_copy(h_hbm.at[0], field.at[(pl.ds(HX, 3), *own)], load_sem.at[1]),
        pltpu.make_async_copy(perm_hbm, field.at[(CO, *own)], load_sem.at[2]),
        pltpu.make_async_copy(fwd_hbm.at[0], fwd, load_sem.at[3]),
        pltpu.make_async_copy(adj_hbm.at[0], adj, load_sem.at[4]),
        pltpu.make_async_copy(pml_hbm, pml_ref, load_sem.at[5]),
        pltpu.make_async_copy(freq_hbm, freq_ref, load_sem.at[6]),
        pltpu.make_async_copy(amp_hbm, amp_ref, load_sem.at[7]),
        pltpu.make_async_copy(blocks_hbm, blocks_ref, load_sem.at[8]),
    ]
    for i in (5, 2, 7, 0, 1, 6, 3, 4, 8):
        loads[i].start()

    for z in (-2, 2, -1, 1):
        tell(barrier, z=z)
    for x in (2, 1, 3):
        tell(barrier, x=x)

    def inside(dx, dy):
        ok = None
        for d, me, n in ((dx, gx, n_x), (dy, gy, n_y)):
            if d != 0:
                here = (me > 0) if d < 0 else (me < n - 1)
                ok = here if ok is None else jnp.logical_and(ok, here)
        return ok

    pl.semaphore_wait(barrier, 17)
    for step in (-2, 2):
        tell(round1, z=step)
        tell(round1, y=step)

    def pick(d, wide):
        if d == 0:
            return pl.ds(0, 16), pl.ds(2, 16)
        if d > 0:
            return pl.ds(16 - wide, wide), pl.ds(2 - wide, wide)
        return pl.ds(0, wide), pl.ds(18, wide)

    e_arg, h_arg = e_hbm.at[0], h_hbm.at[0]
    parts = {
        (1, 0): [(e_arg, EX, 0, 3, 2, 0), (h_arg, HX, 1, 2, 2, 0), (h_arg, HX, 0, 1, 1, 0)],
        (-1, 0): [(e_arg, EX, 1, 2, 2, 0), (h_arg, HX, 0, 3, 1, 0), (e_arg, EX, 0, 1, 1, 0)],
        (0, 1): [(e_arg, EX, 0, 3, 0, 2), (h_arg, HX, 0, 3, 0, 2)],
        (0, -1): [(e_arg, EX, 0, 3, 0, 2), (h_arg, HX, 0, 3, 0, 1)],
        (1, 1): [(e_arg, EX, 0, 3, 1, 1), (h_arg, HX, 0, 3, 1, 1)],
        (1, -1): [(e_arg, EX, 0, 3, 2, 2), (h_arg, HX, 0, 3, 1, 1)],
        (-1, 1): [(e_arg, EX, 0, 3, 2, 2), (h_arg, HX, 0, 3, 1, 1)],
        (-1, -1): [(e_arg, EX, 0, 3, 1, 1)],
    }

    def halo(dx, dy):
        copies = []
        for i, (source, base, first, many, wide_x, wide_y) in enumerate(parts[dx, dy]):
            from_x, to_x = pick(dx, wide_x)
            from_y, to_y = pick(dy, wide_y)
            slot = 3 * sides.index((dx, dy)) + i
            copies.append(
                pltpu.make_async_remote_copy(
                    src_ref=source.at[pl.ds(first, many), from_x, from_y, :],
                    dst_ref=field.at[pl.ds(base + first, many), to_x, to_y, :],
                    send_sem=halo_send.at[slot],
                    recv_sem=halo_recv.at[slot],
                    device_id={"gx": gx + dx, "gy": gy + dy},
                    device_id_type=MESH,
                )
            )
        return copies

    def aux(dx, dy):
        from_x, to_x = pick(dx, 1)
        from_y, to_y = pick(dy, 1)
        slot = 24 + sides.index((dx, dy))
        inner_x = pl.ds(from_x.start + 2, from_x.size)
        inner_y = pl.ds(from_y.start + 2, from_y.size)
        return pltpu.make_async_remote_copy(
            src_ref=field.at[pl.ds(CO, 2), inner_x, inner_y, :],
            dst_ref=field.at[pl.ds(CO, 2), to_x, to_y, :],
            send_sem=halo_send.at[slot],
            recv_sem=halo_recv.at[slot],
            device_id={"gx": gx + dx, "gy": gy + dy},
            device_id_type=MESH,
        )

    order = [(0, 1), (0, -1), (1, 0), (-1, 0), (1, -1), (-1, 1), (1, 1), (-1, -1)]
    aux_order = [side for side in order if side not in ((1, 1), (-1, -1))]

    for dx, dy in order:

        @pl.when(inside(dx, dy))
        def _(dx=dx, dy=dy):
            for copy in halo(dx, dy):
                copy.start()

    def start_aux():
        for dx, dy in aux_order:

            @pl.when(inside(dx, dy))
            def _(dx=dx, dy=dy):
                aux(dx, dy).start()

    @pl.when(gx == 0)
    def _():
        field[:, 0:2] = jnp.zeros((8, 2, ROWS, 128), F32)

    @pl.when(gx == n_x - 1)
    def _():
        field[:, 18:20] = jnp.zeros((8, 2, ROWS, 128), F32)

    @pl.when(gy == 0)
    def _():
        field[:, 0:20, 0:2, :] = jnp.zeros((8, 20, 2, 128), F32)

    @pl.when(gy == n_y - 1)
    def _():
        field[:, 0:20, 18:20, :] = jnp.zeros((8, 20, 2, 128), F32)

    eye = lax.broadcasted_iota(jnp.int32, (16, 16), 0) == lax.broadcasted_iota(
        jnp.int32, (16, 16), 1
    )
    loads[7].wait()
    lane16 = lax.broadcasted_iota(jnp.int32, (16, 128), 1)
    on_plane = lane16 == plane_ref[0]

    def make_drive(x):
        line = jnp.broadcast_to(amp_ref[0, pl.ds(x, 1), :], (16, 16))
        column = jnp.sum(jnp.where(eye, line, 0.0), axis=1, keepdims=True)
        field[DR, x + 2, pl.ds(2, 16), :] = jnp.where(
            on_plane, jnp.broadcast_to(column, (16, 128)), 0.0
        )

    loop(0, 16, 4, make_drive)

    loads[2].wait()

    def make_coef(p):
        field[CO, p, pl.ds(2, 16), :] = courant / field[CO, p, pl.ds(2, 16), :]

    loop(2, 16, 4, make_coef)

    start_aux()

    total_x = n_x * 16
    total_y = n_y * 16

    def profile(cells, total, width):
        place = cells.astype(F32)
        dist = jnp.minimum(place, total - 1.0 - place)
        wide = jnp.full(cells.shape, width, jnp.int32).astype(F32)
        return jnp.maximum(0.0, (wide - dist) / wide) ** 2

    loads[5].wait()
    ys = gy * 16 - 2 + lax.broadcasted_iota(jnp.int32, (ROWS, 128), 0)
    prof_y = profile(ys, total_y, pml_ref[1])
    in_y = (ys >= 0) & (ys < total_y)

    def make_damp(p):
        xs = jnp.full((ROWS, 128), gx * 16 - 2 + p, jnp.int32)
        value = jnp.exp(-absorb * (profile(xs, total_x, pml_ref[0]) + prof_y))
        keep = in_y & (xs >= 0) & (xs < total_x)
        damp[p] = jnp.where(keep, value, 0.0)

    loop(0, 20, 4, make_damp)

    pl.semaphore_wait(round1, 4)
    for x in (2, 1, 3):
        tell(round2, x=x)
    tell(round2, c=1)

    loads[6].wait()
    row_id = lax.broadcasted_iota(jnp.int32, (8, 128), 0)
    tval = (row_id % 2 + 1).astype(F32)
    omega = jnp.where(
        row_id < 2, jnp.full((8, 128), freq_ref[0, 0]), jnp.full((8, 128), freq_ref[0, 1])
    )
    trig[0:8] = jnp.cos(omega * tval)
    trig[8:16] = jnp.sin(omega * tval)

    loads[8].wait()
    loads[3].wait()
    loads[4].wait()

    blocks = blocks_ref[...]
    masks = []
    for bx in range(2):
        for by in range(2):
            cell = (gx * 2 + bx) * (total_y // BS) + gy * 2 + by
            hit = jnp.where(blocks == cell, 1.0, 0.0)
            masks.append(jnp.max(hit, axis=1, keepdims=True))
    upper = lax.broadcasted_iota(jnp.int32, (16, 128), 0) < 8

    def make_weights(bx):
        mask = jnp.where(
            upper,
            jnp.broadcast_to(masks[2 * bx], (16, 128)),
            jnp.broadcast_to(masks[2 * bx + 1], (16, 128)),
        )

        def step(x):
            for k in range(2):
                c1 = trig[pl.ds(2 * k, 1), :]
                c2 = trig[pl.ds(2 * k + 1, 1), :]
                s1 = trig[pl.ds(8 + 2 * k, 1), :]
                s2 = trig[pl.ds(8 + 2 * k + 1, 1), :]
                first = None
                for c in range(3):
                    fr = fwd[k, 0, c, x].astype(F32) * mask
                    fi = fwd[k, 1, c, x].astype(F32) * mask
                    ar = adj[k, 0, c, x].astype(F32)
                    ai = adj[k, 1, c, x].astype(F32)
                    part = fr * ar + fi * ai
                    first = part if first is None else first + part
                    weights[x, k * 7 + 1 + c, pl.ds(2, 16), :] = fr * c1 - fi * s1
                    weights[x, k * 7 + 4 + c, pl.ds(2, 16), :] = fr * c2 - fi * s2
                weights[x, k * 7, pl.ds(2, 16), :] = first

        loop(bx * 8, 8, 1, step)

    make_weights(0)
    make_weights(1)

    loads[0].wait()
    loads[1].wait()

    for dx, dy in order:

        @pl.when(inside(-dx, -dy))
        def _(dx=dx, dy=dy):
            for copy in halo(dx, dy):
                copy.wait_recv()
            if (dx, dy) in aux_order:
                aux(dx, dy).wait_recv()

    lane = lax.broadcasted_iota(jnp.int32, (ROWS, 128), 1)
    not_last = lane < 127
    not_first = lane > 0

    def ahead_z(v):
        return jnp.where(not_last, pltpu.roll(v, 127, 1), 0.0) - v

    def behind_z(v):
        return v - jnp.where(not_first, pltpu.roll(v, 1, 1), 0.0)

    def ahead_y(v):
        return pltpu.roll(v, ROWS - 1, 0) - v

    def behind_y(v):
        return v - pltpu.roll(v, 1, 0)

    def magnetic(p, e, ahead, h):
        d = damp[p]
        ex, ey, ez = e
        hx = d * (h[0] - courant * (ahead_y(ez) - ahead_z(ey)))
        hy = d * (h[1] - courant * (ahead_z(ex) - (ahead[2] - ez)))
        hz = d * (h[2] - courant * ((ahead[1] - ey) - ahead_y(ex)))
        return hx, hy, hz

    def electric(p, h, behind, e, sine):
        d = damp[p]
        co = field[CO, p]
        hx, hy, hz = h
        ex = d * (e[0] + co * (behind_y(hz) - behind_z(hy)))
        ey = d * (e[1] + co * (behind_z(hx) - (hz - behind[2])))
        ez = d * (e[2] + co * ((hy - behind[1]) - behind_y(hx)) + field[DR, p] * sine)
        return ex, ey, ez

    sine1 = trig[pl.ds(8, 1), :]
    sine2 = trig[pl.ds(9, 1), :]

    def read(first, p):
        return tuple(field[first + c, p] for c in range(3))

    others = [(1, 2), (1, 1), (1, 3), (1, 0), (0, 2), (0, 1), (0, 3)]

    def peer(dz, dx):
        return (z_hi + dz) % 2, (lane_x + dx) % 4

    def send_planes(first, count):
        for dz, dx in others:
            k, j = peer(dz, dx)
            pltpu.make_async_remote_copy(
                src_ref=term.at[k, j, pl.ds(first, count), pl.ds(2, 16), :],
                dst_ref=landed.at[grp, pl.ds(first, count)],
                send_sem=red_send,
                recv_sem=red_recv,
                device_id={"grp": k * 4 + j},
                device_id_type=MESH,
            ).start()

    e0 = read(EX, 0)
    h1 = e1 = h2 = None
    for p in range(19):
        e0_next = read(EX, p + 1)
        h1_last, e1_last, h2_last = h1, e1, h2
        h1 = magnetic(p, e0, e0_next, read(HX, p))
        if p >= 1:
            e1 = electric(p, h1, h1_last, e0, sine1)
        if p >= 2:
            h2 = magnetic(p - 1, e1_last, e1, h1_last)
        if p >= 3:
            e2 = electric(p - 1, h2, h2_last, e1_last, sine2)
            x = p - 3
            for k in range(2):
                value = weights[x, k * 7]
                for c in range(3):
                    value = value + weights[x, k * 7 + 1 + c] * e1_last[c]
                    value = value + weights[x, k * 7 + 4 + c] * e2[c]
                term[k, x % 4, x // 4] = value
            if x == READY[0]:
                pl.semaphore_wait(round2, 4)
            if x in READY:
                first = 0 if x == READY[0] else 1 + READY[READY.index(x) - 1] // 4
                send_planes(first, x // 4 + 1 - first)
        e0 = e0_next

    landed[grp] = term[z_hi, lane_x, :, 2:18, :]
    seven = landed.at[pl.ds(0, 7)]
    pltpu.make_async_copy(seven, seven, red_recv).wait()

    total = landed[0]
    for j in range(1, 8):
        total = total + landed[j]
    summed[...] = total
    square = jnp.sum(total * total, axis=0)
    line = jnp.sum(square, axis=0, keepdims=True)

    me1 = lane_x * 8 + gy
    me2 = z_hi * 8 + gx
    row1[...] = line
    rows1[pl.ds(me1, 1), :] = line
    steps = [(dx, dy) for dx in range(4) for dy in range(8) if (dx, dy) != (0, 0)]
    for dx, dy in sorted(steps, key=lambda d: -min(d[0], 4 - d[0]) - min(d[1], 8 - d[1])):
        pltpu.make_async_remote_copy(
            src_ref=row1,
            dst_ref=rows1.at[pl.ds(me1, 1)],
            send_sem=s1_send,
            recv_sem=s1_recv,
            device_id={"grp": z_hi * 4 + (lane_x + dx) % 4, "gy": (gy + dy) % 8},
            device_id_type=MESH,
        ).start()

    mine = grad_out.at[z_hi, :, lane_x]
    out = pltpu.make_async_copy(summed, mine, out_sem)
    out.start()
    for dz, dx in others:
        k, j = peer(dz, dx)
        pltpu.make_async_remote_copy(
            src_ref=summed,
            dst_ref=mine,
            send_sem=gat_send,
            recv_sem=gat_recv,
            device_id={"grp": k * 4 + j},
            device_id_type=MESH,
        ).start()

    some = rows1.at[pl.ds(0, 31)]
    pltpu.make_async_copy(some, some, s1_recv).wait()
    line = jnp.sum(rows1[...], axis=0, keepdims=True)
    row2[...] = line
    rows2[pl.ds(me2, 1), :] = line
    steps = [(dz, dc) for dz in range(8) for dc in range(2) if (dz, dc) != (0, 0)]
    for dz, dc in sorted(steps, key=lambda d: -min(d[0], 8 - d[0])):
        to_z = (place + dz) % 8
        pltpu.make_async_remote_copy(
            src_ref=row2,
            dst_ref=rows2.at[pl.ds(me2, 1)],
            send_sem=s2_send,
            recv_sem=s2_recv,
            device_id={
                "grp": (to_z // 4) * 4 + lane_x,
                "gx": (to_z % 4) * 2 + (gx + dc) % 2,
            },
            device_id_type=MESH,
        ).start()

    for dx, dy in order:

        @pl.when(inside(dx, dy))
        def _(dx=dx, dy=dy):
            for copy in halo(dx, dy):
                copy.wait_send()
            if (dx, dy) in aux_order:
                aux(dx, dy).wait_send()

    pltpu.make_async_copy(seven, seven, red_send).wait()
    pltpu.make_async_copy(seven, seven, gat_send).wait()
    pltpu.make_async_copy(some, some, s1_send).wait()
    out.wait()
    pltpu.make_async_copy(seven, seven, gat_recv).wait()

    few = rows2.at[pl.ds(0, 15)]
    pltpu.make_async_copy(few, few, s2_recv).wait()
    count = float(128 * BS * BS * 128)
    for k in range(2):
        squares = jnp.sum(rows2[8 * k : 8 * k + 8], axis=0, keepdims=True)
        squares = jnp.sum(squares, axis=1, keepdims=True)
        value = lax.rsqrt(squares / count + 1e-05)
        scale_ref[k] = jnp.broadcast_to(value, (8, 128))
    pltpu.make_async_copy(few, few, s2_send).wait()


def body(
    efield,
    hfield,
    fwd_dft,
    adj_dft,
    permittivity,
    source_amp,
    source_plane,
    freqs,
    pml_width,
    design_blocks,
):
    hbm = pl.BlockSpec(memory_space=pltpu.HBM)
    def pin(value):
        return pltpu.with_memory_space_constraint(value, pltpu.HBM)

    vmem = pl.BlockSpec(memory_space=pltpu.VMEM)
    dma = pltpu.SemaphoreType.DMA
    grad, scale = pl.pallas_call(
        kernel,
        out_shape=(
            jax.ShapeDtypeStruct((2, 4, 4, 16, 128), F32),
            jax.ShapeDtypeStruct((2, 8, 128), F32),
        ),
        in_specs=[hbm] * 6 + [pl.BlockSpec(memory_space=pltpu.SMEM)] + [hbm] * 3,
        out_specs=(pl.BlockSpec(memory_space=pl.ANY), vmem),
        scratch_shapes=[
            pltpu.VMEM((8, PLANES, ROWS, 128), F32),
            pltpu.VMEM((20, ROWS, 128), F32),
            pltpu.VMEM((2, 2, 3, 16, 16, 128), jnp.bfloat16),
            pltpu.VMEM((2, 2, 3, 16, 16, 128), jnp.bfloat16),
            pltpu.VMEM((16, 128), F32),
            pltpu.VMEM((16, 14, ROWS, 128), F32),
            pltpu.VMEM((2, 4, 4, ROWS, 128), F32),
            pltpu.VMEM((8, 4, 16, 128), F32),
            pltpu.VMEM((4, 16, 128), F32),
            pltpu.VMEM((1, 128), F32),
            pltpu.VMEM((32, 128), F32),
            pltpu.VMEM((1, 128), F32),
            pltpu.VMEM((16, 128), F32),
            pltpu.VMEM((1, 16, 16), F32),
            pltpu.SMEM((1, 2), F32),
            pltpu.SMEM((2,), jnp.int32),
            pltpu.VMEM((1, 128), jnp.int32),
            dma((9,)),
            dma((32,)),
            dma((32,)),
            dma,
            dma,
            dma,
            dma,
            dma,
            dma,
            dma,
            dma,
            dma,
            pltpu.SemaphoreType.REGULAR,
            pltpu.SemaphoreType.REGULAR,
        ],
        compiler_params=pltpu.CompilerParams(
            collective_id=0, has_side_effects=True, vmem_limit_bytes=40 * 1024 * 1024
        ),
        name="adjoint",
    )(
        *map(pin, (efield, hfield, fwd_dft, adj_dft, permittivity, source_amp)),
        source_plane,
        *map(pin, (freqs, pml_width, design_blocks[None, :])),
    )
    return grad.reshape(2, 16, 16, 128) * scale[:, :1, None, :]


def solution(mesh):
    in_specs = (
        P("grp", None, "gx", "gy", None),
        P("grp", None, "gx", "gy", None),
        P("grp", None, None, None, "gx", "gy", None),
        P("grp", None, None, None, "gx", "gy", None),
        P("gx", "gy", None),
        P("grp", "gx", "gy"),
        P("grp"),
        P("grp", None),
        P(),
        P(),
    )
    out_specs = P(None, "gx", "gy", None)
    return jax.shard_map(body, mesh=mesh, in_specs=in_specs, out_specs=out_specs, check_vma=False)
```

```python
import functools

import jax
import jax.numpy as jnp
from jax import lax
from jax.experimental import pallas as pl
from jax.experimental.pallas import tpu as pltpu
from jax.sharding import PartitionSpec as P

BS = 8
MESH = pl.DeviceIdType.MESH
F32 = jnp.float32

courant = 0.5
absorb = 0.8

PLANES = 21
ROWS = 24
READY = (7, 15)
EX, EY, EZ, HX, HY, HZ, CO, DR = range(8)


def loop(low, count, unroll, step):
    assert count % unroll == 0

    def body(i, carry):
        for u in range(unroll):
            step(low + i * unroll + u)
        return carry

    lax.fori_loop(0, count // unroll, body, 0)


def kernel(
    e_hbm,
    h_hbm,
    fwd_hbm,
    adj_hbm,
    perm_hbm,
    amp_hbm,
    plane_ref,
    freq_hbm,
    pml_hbm,
    blocks_hbm,
    grad_out,
    scale_ref,
    field,
    damp,
    fwd,
    adj,
    trig,
    weights,
    term,
    landed,
    summed,
    row1,
    rows1,
    row2,
    rows2,
    amp_ref,
    freq_ref,
    pml_ref,
    blocks_ref,
    load_sem,
    halo_send,
    halo_recv,
    red_send,
    red_recv,
    gat_send,
    gat_recv,
    s1_send,
    s1_recv,
    s2_send,
    s2_recv,
    out_sem,
    round1,
    round2,
):
    grp = lax.axis_index("grp")
    gx = lax.axis_index("gx")
    gy = lax.axis_index("gy")
    z_hi = grp // 4
    n_x = 8
    n_y = 8

    lane_x = grp % 4
    z_lo = gx // 2
    core = gx % 2
    place = z_hi * 4 + z_lo
    sides = [(dx, dy) for dx in (-1, 0, 1) for dy in (-1, 0, 1) if (dx, dy) != (0, 0)]

    def device(x=0, y=0, z=0, c=0):
        there = (place + z) % 8
        return {
            "grp": (there // 4) * 4 + (lane_x + x) % 4,
            "gx": (there % 4) * 2 + (core + c) % 2,
            "gy": (gy + y) % 8,
        }

    def tell(semaphore, **steps):
        pl.semaphore_signal(
            semaphore, inc=1, device_id=device(**steps), device_id_type=MESH
        )

    barrier = pltpu.get_barrier_semaphore()
    beyond = 2 * core - 1
    for y in (-1, 1, 0):
        tell(barrier, y=y, z=beyond, c=1)
    for y in (-1, 1, 0):
        tell(barrier, y=y, c=1)
    for y in (-1, 1, -2, 2):
        tell(barrier, y=y)

    own = (pl.ds(2, 16), pl.ds(2, 16))
    loads = [
        pltpu.make_async_copy(e_hbm.at[0], field.at[(pl.ds(EX, 3), *own)], load_sem.at[0]),
        pltpu.make_async_copy(h_hbm.at[0], field.at[(pl.ds(HX, 3), *own)], load_sem.at[1]),
        pltpu.make_async_copy(perm_hbm, field.at[(CO, *own)], load_sem.at[2]),
        pltpu.make_async_copy(fwd_hbm.at[0], fwd, load_sem.at[3]),
        pltpu.make_async_copy(adj_hbm.at[0], adj, load_sem.at[4]),
        pltpu.make_async_copy(pml_hbm, pml_ref, load_sem.at[5]),
        pltpu.make_async_copy(freq_hbm, freq_ref, load_sem.at[6]),
        pltpu.make_async_copy(amp_hbm, amp_ref, load_sem.at[7]),
        pltpu.make_async_copy(blocks_hbm, blocks_ref, load_sem.at[8]),
    ]
    for i in (5, 2, 7, 0, 1, 6, 3, 4, 8):
        loads[i].start()

    for z in (-2, 2, -1, 1):
        tell(barrier, z=z)
    for x in (2, 1, 3):
        tell(barrier, x=x)

    def inside(dx, dy):
        ok = None
        for d, me, n in ((dx, gx, n_x), (dy, gy, n_y)):
            if d != 0:
                here = (me > 0) if d < 0 else (me < n - 1)
                ok = here if ok is None else jnp.logical_and(ok, here)
        return ok

    pl.semaphore_wait(barrier, 17)
    for step in (-2, 2):
        tell(round1, z=step)
        tell(round1, y=step)

    def pick(d, wide):
        if d == 0:
            return pl.ds(0, 16), pl.ds(2, 16)
        if d > 0:
            return pl.ds(16 - wide, wide), pl.ds(2 - wide, wide)
        return pl.ds(0, wide), pl.ds(18, wide)

    e_arg, h_arg = e_hbm.at[0], h_hbm.at[0]
    parts = {
        (1, 0): [(e_arg, EX, 0, 3, 2, 0), (h_arg, HX, 1, 2, 2, 0), (h_arg, HX, 0, 1, 1, 0)],
        (-1, 0): [(e_arg, EX, 1, 2, 2, 0), (h_arg, HX, 0, 3, 1, 0), (e_arg, EX, 0, 1, 1, 0)],
        (0, 1): [(e_arg, EX, 0, 3, 0, 2), (h_arg, HX, 0, 3, 0, 2)],
        (0, -1): [(e_arg, EX, 0, 3, 0, 2), (h_arg, HX, 0, 3, 0, 1)],
        (1, 1): [(e_arg, EX, 0, 3, 1, 1), (h_arg, HX, 0, 3, 1, 1)],
        (1, -1): [(e_arg, EX, 0, 3, 2, 2), (h_arg, HX, 0, 3, 1, 1)],
        (-1, 1): [(e_arg, EX, 0, 3, 2, 2), (h_arg, HX, 0, 3, 1, 1)],
        (-1, -1): [(e_arg, EX, 0, 3, 1, 1)],
    }

    def halo(dx, dy):
        copies = []
        for i, (source, base, first, many, wide_x, wide_y) in enumerate(parts[dx, dy]):
            from_x, to_x = pick(dx, wide_x)
            from_y, to_y = pick(dy, wide_y)
            slot = 3 * sides.index((dx, dy)) + i
            copies.append(
                pltpu.make_async_remote_copy(
                    src_ref=source.at[pl.ds(first, many), from_x, from_y, :],
                    dst_ref=field.at[pl.ds(base + first, many), to_x, to_y, :],
                    send_sem=halo_send.at[slot],
                    recv_sem=halo_recv.at[slot],
                    device_id={"gx": gx + dx, "gy": gy + dy},
                    device_id_type=MESH,
                )
            )
        return copies

    def aux(dx, dy):
        from_x, to_x = pick(dx, 1)
        from_y, to_y = pick(dy, 1)
        slot = 24 + sides.index((dx, dy))
        inner_x = pl.ds(from_x.start + 2, from_x.size)
        inner_y = pl.ds(from_y.start + 2, from_y.size)
        return pltpu.make_async_remote_copy(
            src_ref=field.at[pl.ds(CO, 2), inner_x, inner_y, :],
            dst_ref=field.at[pl.ds(CO, 2), to_x, to_y, :],
            send_sem=halo_send.at[slot],
            recv_sem=halo_recv.at[slot],
            device_id={"gx": gx + dx, "gy": gy + dy},
            device_id_type=MESH,
        )

    order = [(0, 1), (0, -1), (1, 0), (-1, 0), (1, -1), (-1, 1), (1, 1), (-1, -1)]
    aux_order = [side for side in order if side not in ((1, 1), (-1, -1))]

    for dx, dy in order:

        @pl.when(inside(dx, dy))
        def _(dx=dx, dy=dy):
            for copy in halo(dx, dy):
                copy.start()

    def start_aux():
        for dx, dy in aux_order:

            @pl.when(inside(dx, dy))
            def _(dx=dx, dy=dy):
                aux(dx, dy).start()

    @pl.when(gx == 0)
    def _():
        field[:, 0:2] = jnp.zeros((8, 2, ROWS, 128), F32)

    @pl.when(gx == n_x - 1)
    def _():
        field[:, 18:20] = jnp.zeros((8, 2, ROWS, 128), F32)

    @pl.when(gy == 0)
    def _():
        field[:, 0:20, 0:2, :] = jnp.zeros((8, 20, 2, 128), F32)

    @pl.when(gy == n_y - 1)
    def _():
        field[:, 0:20, 18:20, :] = jnp.zeros((8, 20, 2, 128), F32)

    eye = lax.broadcasted_iota(jnp.int32, (16, 16), 0) == lax.broadcasted_iota(
        jnp.int32, (16, 16), 1
    )
    loads[7].wait()
    lane16 = lax.broadcasted_iota(jnp.int32, (16, 128), 1)
    on_plane = lane16 == plane_ref[0]

    def make_drive(x):
        line = jnp.broadcast_to(amp_ref[0, pl.ds(x, 1), :], (16, 16))
        column = jnp.sum(jnp.where(eye, line, 0.0), axis=1, keepdims=True)
        field[DR, x + 2, pl.ds(2, 16), :] = jnp.where(
            on_plane, jnp.broadcast_to(column, (16, 128)), 0.0
        )

    loop(0, 16, 4, make_drive)

    loads[2].wait()

    def make_coef(p):
        field[CO, p, pl.ds(2, 16), :] = courant / field[CO, p, pl.ds(2, 16), :]

    loop(2, 16, 4, make_coef)

    start_aux()

    total_x = n_x * 16
    total_y = n_y * 16

    def profile(cells, total, width):
        place = cells.astype(F32)
        dist = jnp.minimum(place, total - 1.0 - place)
        wide = jnp.full(cells.shape, width, jnp.int32).astype(F32)
        return jnp.maximum(0.0, (wide - dist) / wide) ** 2

    loads[5].wait()
    ys = gy * 16 - 2 + lax.broadcasted_iota(jnp.int32, (ROWS, 128), 0)
    prof_y = profile(ys, total_y, pml_ref[1])
    in_y = (ys >= 0) & (ys < total_y)

    def make_damp(p):
        xs = jnp.full((ROWS, 128), gx * 16 - 2 + p, jnp.int32)
        value = jnp.exp(-absorb * (profile(xs, total_x, pml_ref[0]) + prof_y))
        keep = in_y & (xs >= 0) & (xs < total_x)
        damp[p] = jnp.where(keep, value, 0.0)

    loop(0, 20, 4, make_damp)

    pl.semaphore_wait(round1, 4)
    for x in (2, 1, 3):
        tell(round2, x=x)
    tell(round2, c=1)

    loads[6].wait()
    row_id = lax.broadcasted_iota(jnp.int32, (8, 128), 0)
    tval = (row_id % 2 + 1).astype(F32)
    omega = jnp.where(
        row_id < 2, jnp.full((8, 128), freq_ref[0, 0]), jnp.full((8, 128), freq_ref[0, 1])
    )
    trig[0:8] = jnp.cos(omega * tval)
    trig[8:16] = jnp.sin(omega * tval)

    loads[8].wait()
    loads[3].wait()
    loads[4].wait()

    blocks = blocks_ref[...]
    masks = []
    for bx in range(2):
        for by in range(2):
            cell = (gx * 2 + bx) * (total_y // BS) + gy * 2 + by
            hit = jnp.where(blocks == cell, 1.0, 0.0)
            masks.append(jnp.max(hit, axis=1, keepdims=True))
    upper = lax.broadcasted_iota(jnp.int32, (16, 128), 0) < 8

    def make_weights(bx):
        mask = jnp.where(
            upper,
            jnp.broadcast_to(masks[2 * bx], (16, 128)),
            jnp.broadcast_to(masks[2 * bx + 1], (16, 128)),
        )

        def step(x):
            for k in range(2):
                c1 = trig[pl.ds(2 * k, 1), :]
                c2 = trig[pl.ds(2 * k + 1, 1), :]
                s1 = trig[pl.ds(8 + 2 * k, 1), :]
                s2 = trig[pl.ds(8 + 2 * k + 1, 1), :]
                first = None
                for c in range(3):
                    fr = fwd[k, 0, c, x].astype(F32) * mask
                    fi = fwd[k, 1, c, x].astype(F32) * mask
                    ar = adj[k, 0, c, x].astype(F32)
                    ai = adj[k, 1, c, x].astype(F32)
                    part = fr * ar + fi * ai
                    first = part if first is None else first + part
                    weights[x, k * 7 + 1 + c, pl.ds(2, 16), :] = fr * c1 - fi * s1
                    weights[x, k * 7 + 4 + c, pl.ds(2, 16), :] = fr * c2 - fi * s2
                weights[x, k * 7, pl.ds(2, 16), :] = first

        loop(bx * 8, 8, 1, step)

    make_weights(0)
    make_weights(1)

    loads[0].wait()
    loads[1].wait()

    for dx, dy in order:

        @pl.when(inside(-dx, -dy))
        def _(dx=dx, dy=dy):
            for copy in halo(dx, dy):
                copy.wait_recv()
            if (dx, dy) in aux_order:
                aux(dx, dy).wait_recv()

    lane = lax.broadcasted_iota(jnp.int32, (ROWS, 128), 1)
    not_last = lane < 127
    not_first = lane > 0

    def ahead_z(v):
        return jnp.where(not_last, pltpu.roll(v, 127, 1), 0.0) - v

    def behind_z(v):
        return v - jnp.where(not_first, pltpu.roll(v, 1, 1), 0.0)

    def ahead_y(v):
        return pltpu.roll(v, ROWS - 1, 0) - v

    def behind_y(v):
        return v - pltpu.roll(v, 1, 0)

    def magnetic(p, e, ahead, h):
        d = damp[p]
        ex, ey, ez = e
        hx = d * (h[0] - courant * (ahead_y(ez) - ahead_z(ey)))
        hy = d * (h[1] - courant * (ahead_z(ex) - (ahead[2] - ez)))
        hz = d * (h[2] - courant * ((ahead[1] - ey) - ahead_y(ex)))
        return hx, hy, hz

    def electric(p, h, behind, e, sine):
        d = damp[p]
        co = field[CO, p]
        hx, hy, hz = h
        ex = d * (e[0] + co * (behind_y(hz) - behind_z(hy)))
        ey = d * (e[1] + co * (behind_z(hx) - (hz - behind[2])))
        ez = d * (e[2] + co * ((hy - behind[1]) - behind_y(hx)) + field[DR, p] * sine)
        return ex, ey, ez

    sine1 = trig[pl.ds(8, 1), :]
    sine2 = trig[pl.ds(9, 1), :]

    def read(first, p):
        return tuple(field[first + c, p] for c in range(3))

    others = [(1, 2), (1, 1), (1, 3), (1, 0), (0, 2), (0, 1), (0, 3)]

    def peer(dz, dx):
        return (z_hi + dz) % 2, (lane_x + dx) % 4

    def send_planes(first, count):
        for dz, dx in others:
            k, j = peer(dz, dx)
            pltpu.make_async_remote_copy(
                src_ref=term.at[k, j, pl.ds(first, count), pl.ds(2, 16), :],
                dst_ref=landed.at[grp, pl.ds(first, count)],
                send_sem=red_send,
                recv_sem=red_recv,
                device_id={"grp": k * 4 + j},
                device_id_type=MESH,
            ).start()

    e0 = read(EX, 0)
    h1 = e1 = h2 = None
    for p in range(19):
        e0_next = read(EX, p + 1)
        h1_last, e1_last, h2_last = h1, e1, h2
        h1 = magnetic(p, e0, e0_next, read(HX, p))
        if p >= 1:
            e1 = electric(p, h1, h1_last, e0, sine1)
        if p >= 2:
            h2 = magnetic(p - 1, e1_last, e1, h1_last)
        if p >= 3:
            e2 = electric(p - 1, h2, h2_last, e1_last, sine2)
            x = p - 3
            for k in range(2):
                value = weights[x, k * 7]
                for c in range(3):
                    value = value + weights[x, k * 7 + 1 + c] * e1_last[c]
                    value = value + weights[x, k * 7 + 4 + c] * e2[c]
                term[k, x % 4, x // 4] = value
            if x == READY[0]:
                pl.semaphore_wait(round2, 4)
            if x in READY:
                first = 0 if x == READY[0] else 1 + READY[READY.index(x) - 1] // 4
                send_planes(first, x // 4 + 1 - first)
        e0 = e0_next

    landed[grp] = term[z_hi, lane_x, :, 2:18, :]
    seven = landed.at[pl.ds(0, 7)]
    pltpu.make_async_copy(seven, seven, red_recv).wait()

    total = landed[0]
    for j in range(1, 8):
        total = total + landed[j]
    summed[...] = total
    square = jnp.sum(total * total, axis=0)
    line = jnp.sum(square, axis=0, keepdims=True)

    me1 = gy * 2 + core
    me2 = place * 4 + lane_x
    row1[...] = line
    rows1[pl.ds(me1, 1), :] = line
    steps = [(dy, dc) for dy in range(8) for dc in range(2) if (dy, dc) != (0, 0)]
    for dy, dc in sorted(steps, key=lambda d: -min(d[0], 8 - d[0])):
        pltpu.make_async_remote_copy(
            src_ref=row1,
            dst_ref=rows1.at[pl.ds(me1, 1)],
            send_sem=s1_send,
            recv_sem=s1_recv,
            device_id=device(y=dy, c=dc),
            device_id_type=MESH,
        ).start()

    mine = grad_out.at[z_hi, :, lane_x]
    out = pltpu.make_async_copy(summed, mine, out_sem)
    out.start()
    for dz, dx in others:
        k, j = peer(dz, dx)
        pltpu.make_async_remote_copy(
            src_ref=summed,
            dst_ref=mine,
            send_sem=gat_send,
            recv_sem=gat_recv,
            device_id={"grp": k * 4 + j},
            device_id_type=MESH,
        ).start()

    some = rows1.at[pl.ds(0, 15)]
    pltpu.make_async_copy(some, some, s1_recv).wait()
    line = jnp.sum(rows1[...], axis=0, keepdims=True)
    row2[...] = line
    rows2[pl.ds(me2, 1), :] = line
    steps = [(dz, dx) for dz in range(8) for dx in range(4) if (dz, dx) != (0, 0)]
    for dz, dx in sorted(steps, key=lambda d: -min(d[0], 8 - d[0]) - min(d[1], 4 - d[1])):
        pltpu.make_async_remote_copy(
            src_ref=row2,
            dst_ref=rows2.at[pl.ds(me2, 1)],
            send_sem=s2_send,
            recv_sem=s2_recv,
            device_id=device(z=dz, x=dx),
            device_id_type=MESH,
        ).start()

    for dx, dy in order:

        @pl.when(inside(dx, dy))
        def _(dx=dx, dy=dy):
            for copy in halo(dx, dy):
                copy.wait_send()
            if (dx, dy) in aux_order:
                aux(dx, dy).wait_send()

    pltpu.make_async_copy(seven, seven, red_send).wait()
    pltpu.make_async_copy(seven, seven, gat_send).wait()
    pltpu.make_async_copy(some, some, s1_send).wait()
    out.wait()
    pltpu.make_async_copy(seven, seven, gat_recv).wait()

    few = rows2.at[pl.ds(0, 31)]
    pltpu.make_async_copy(few, few, s2_recv).wait()
    count = float(128 * BS * BS * 128)
    for k in range(2):
        squares = jnp.sum(rows2[16 * k : 16 * k + 16], axis=0, keepdims=True)
        squares = jnp.sum(squares, axis=1, keepdims=True)
        value = lax.rsqrt(squares / count + 1e-05)
        scale_ref[k] = jnp.broadcast_to(value, (8, 128))
    pltpu.make_async_copy(few, few, s2_send).wait()


def body(
    efield,
    hfield,
    fwd_dft,
    adj_dft,
    permittivity,
    source_amp,
    source_plane,
    freqs,
    pml_width,
    design_blocks,
):
    hbm = pl.BlockSpec(memory_space=pltpu.HBM)
    def pin(value):
        return pltpu.with_memory_space_constraint(value, pltpu.HBM)

    vmem = pl.BlockSpec(memory_space=pltpu.VMEM)
    dma = pltpu.SemaphoreType.DMA
    grad, scale = pl.pallas_call(
        kernel,
        out_shape=(
            jax.ShapeDtypeStruct((2, 4, 4, 16, 128), F32),
            jax.ShapeDtypeStruct((2, 8, 128), F32),
        ),
        in_specs=[hbm] * 6 + [pl.BlockSpec(memory_space=pltpu.SMEM)] + [hbm] * 3,
        out_specs=(pl.BlockSpec(memory_space=pl.ANY), vmem),
        scratch_shapes=[
            pltpu.VMEM((8, PLANES, ROWS, 128), F32),
            pltpu.VMEM((20, ROWS, 128), F32),
            pltpu.VMEM((2, 2, 3, 16, 16, 128), jnp.bfloat16),
            pltpu.VMEM((2, 2, 3, 16, 16, 128), jnp.bfloat16),
            pltpu.VMEM((16, 128), F32),
            pltpu.VMEM((16, 14, ROWS, 128), F32),
            pltpu.VMEM((2, 4, 4, ROWS, 128), F32),
            pltpu.VMEM((8, 4, 16, 128), F32),
            pltpu.VMEM((4, 16, 128), F32),
            pltpu.VMEM((1, 128), F32),
            pltpu.VMEM((16, 128), F32),
            pltpu.VMEM((1, 128), F32),
            pltpu.VMEM((32, 128), F32),
            pltpu.VMEM((1, 16, 16), F32),
            pltpu.SMEM((1, 2), F32),
            pltpu.SMEM((2,), jnp.int32),
            pltpu.VMEM((1, 128), jnp.int32),
            dma((9,)),
            dma((32,)),
            dma((32,)),
            dma,
            dma,
            dma,
            dma,
            dma,
            dma,
            dma,
            dma,
            dma,
            pltpu.SemaphoreType.REGULAR,
            pltpu.SemaphoreType.REGULAR,
        ],
        compiler_params=pltpu.CompilerParams(
            collective_id=0, has_side_effects=True, vmem_limit_bytes=40 * 1024 * 1024
        ),
        name="adjoint",
    )(
        *map(pin, (efield, hfield, fwd_dft, adj_dft, permittivity, source_amp)),
        source_plane,
        *map(pin, (freqs, pml_width, design_blocks[None, :])),
    )
    return grad.reshape(2, 16, 16, 128) * scale[:, :1, None, :]


def solution(mesh):
    in_specs = (
        P("grp", None, "gx", "gy", None),
        P("grp", None, "gx", "gy", None),
        P("grp", None, None, None, "gx", "gy", None),
        P("grp", None, None, None, "gx", "gy", None),
        P("gx", "gy", None),
        P("grp", "gx", "gy"),
        P("grp"),
        P("grp", None),
        P(),
        P(),
    )
    out_specs = P(None, "gx", "gy", None)
    return jax.shard_map(body, mesh=mesh, in_specs=in_specs, out_specs=out_specs, check_vma=False)
```

```python
import functools

import jax
import jax.numpy as jnp
from jax import lax
from jax.experimental import pallas as pl
from jax.experimental.pallas import tpu as pltpu
from jax.sharding import PartitionSpec as P

BS = 8
MESH = pl.DeviceIdType.MESH
F32 = jnp.float32

courant = 0.5
absorb = 0.8

PLANES = 21
ROWS = 24
READY = (7, 15)
EX, EY, EZ, HX, HY, HZ, CO, DR = range(8)


def loop(low, count, unroll, step):
    assert count % unroll == 0

    def body(i, carry):
        for u in range(unroll):
            step(low + i * unroll + u)
        return carry

    lax.fori_loop(0, count // unroll, body, 0)


def kernel(
    e_hbm,
    h_hbm,
    fwd_hbm,
    adj_hbm,
    perm_hbm,
    amp_hbm,
    plane_ref,
    freq_hbm,
    pml_hbm,
    blocks_hbm,
    grad_out,
    scale_ref,
    field,
    damp,
    fwd,
    adj,
    trig,
    weights,
    term,
    landed,
    summed,
    row1,
    rows1,
    row2,
    rows2,
    amp_ref,
    freq_ref,
    pml_ref,
    blocks_ref,
    load_sem,
    halo_send,
    halo_recv,
    red_send,
    red_recv,
    gat_send,
    gat_recv,
    s1_send,
    s1_recv,
    s2_send,
    s2_recv,
    out_sem,
    round1,
    round2,
):
    grp = lax.axis_index("grp")
    gx = lax.axis_index("gx")
    gy = lax.axis_index("gy")
    z_hi = grp // 4
    n_x = 8
    n_y = 8

    lane_x = grp % 4
    z_lo = gx // 2
    core = gx % 2
    place = z_hi * 4 + z_lo
    sides = [(dx, dy) for dx in (-1, 0, 1) for dy in (-1, 0, 1) if (dx, dy) != (0, 0)]

    def device(x=0, y=0, z=0, c=0):
        there = (place + z) % 8
        return {
            "grp": (there // 4) * 4 + (lane_x + x) % 4,
            "gx": (there % 4) * 2 + (core + c) % 2,
            "gy": (gy + y) % 8,
        }

    def tell(semaphore, **steps):
        pl.semaphore_signal(
            semaphore, inc=1, device_id=device(**steps), device_id_type=MESH
        )

    barrier = pltpu.get_barrier_semaphore()
    beyond = 2 * core - 1
    for y in (-1, 1, 0):
        tell(barrier, y=y, z=beyond, c=1)
    for y in (-1, 1, 0):
        tell(barrier, y=y, c=1)
    for y in (-1, 1, -2, 2):
        tell(barrier, y=y)

    own = (pl.ds(2, 16), pl.ds(2, 16))
    loads = [
        pltpu.make_async_copy(e_hbm.at[0], field.at[(pl.ds(EX, 3), *own)], load_sem.at[0]),
        pltpu.make_async_copy(h_hbm.at[0], field.at[(pl.ds(HX, 3), *own)], load_sem.at[1]),
        pltpu.make_async_copy(perm_hbm, field.at[(CO, *own)], load_sem.at[2]),
        pltpu.make_async_copy(fwd_hbm.at[0], fwd, load_sem.at[3]),
        pltpu.make_async_copy(adj_hbm.at[0], adj, load_sem.at[4]),
        pltpu.make_async_copy(pml_hbm, pml_ref, load_sem.at[5]),
        pltpu.make_async_copy(freq_hbm, freq_ref, load_sem.at[6]),
        pltpu.make_async_copy(amp_hbm, amp_ref, load_sem.at[7]),
        pltpu.make_async_copy(blocks_hbm, blocks_ref, load_sem.at[8]),
    ]
    for i in (5, 2, 7, 0, 1, 6, 3, 4, 8):
        loads[i].start()

    for z in (-2, 2, -1, 1):
        tell(barrier, z=z)
    for x in (2, 1, 3):
        tell(barrier, x=x)

    def inside(dx, dy):
        ok = None
        for d, me, n in ((dx, gx, n_x), (dy, gy, n_y)):
            if d != 0:
                here = (me > 0) if d < 0 else (me < n - 1)
                ok = here if ok is None else jnp.logical_and(ok, here)
        return ok

    pl.semaphore_wait(barrier, 17)
    for step in (-2, 2):
        tell(round1, z=step)
        tell(round1, y=step)

    def pick(d, wide):
        if d == 0:
            return pl.ds(0, 16), pl.ds(2, 16)
        if d > 0:
            return pl.ds(16 - wide, wide), pl.ds(2 - wide, wide)
        return pl.ds(0, wide), pl.ds(18, wide)

    e_arg, h_arg = e_hbm.at[0], h_hbm.at[0]
    parts = {
        (1, 0): [(e_arg, EX, 0, 3, 2, 0), (h_arg, HX, 1, 2, 2, 0), (h_arg, HX, 0, 1, 1, 0)],
        (-1, 0): [(e_arg, EX, 1, 2, 2, 0), (h_arg, HX, 0, 3, 1, 0), (e_arg, EX, 0, 1, 1, 0)],
        (0, 1): [(e_arg, EX, 0, 3, 0, 2), (h_arg, HX, 0, 3, 0, 2)],
        (0, -1): [(e_arg, EX, 0, 3, 0, 2), (h_arg, HX, 0, 3, 0, 1)],
        (1, 1): [(e_arg, EX, 0, 3, 1, 1), (h_arg, HX, 0, 3, 1, 1)],
        (1, -1): [(e_arg, EX, 0, 3, 2, 2), (h_arg, HX, 0, 3, 1, 1)],
        (-1, 1): [(e_arg, EX, 0, 3, 2, 2), (h_arg, HX, 0, 3, 1, 1)],
        (-1, -1): [(e_arg, EX, 0, 3, 1, 1)],
    }

    def halo(dx, dy):
        copies = []
        for i, (source, base, first, many, wide_x, wide_y) in enumerate(parts[dx, dy]):
            from_x, to_x = pick(dx, wide_x)
            from_y, to_y = pick(dy, wide_y)
            slot = 3 * sides.index((dx, dy)) + i
            copies.append(
                pltpu.make_async_remote_copy(
                    src_ref=source.at[pl.ds(first, many), from_x, from_y, :],
                    dst_ref=field.at[pl.ds(base + first, many), to_x, to_y, :],
                    send_sem=halo_send.at[slot],
                    recv_sem=halo_recv.at[slot],
                    device_id={"gx": gx + dx, "gy": gy + dy},
                    device_id_type=MESH,
                )
            )
        return copies

    def aux(dx, dy):
        from_x, to_x = pick(dx, 1)
        from_y, to_y = pick(dy, 1)
        slot = 24 + sides.index((dx, dy))
        inner_x = pl.ds(from_x.start + 2, from_x.size)
        inner_y = pl.ds(from_y.start + 2, from_y.size)
        return pltpu.make_async_remote_copy(
            src_ref=field.at[pl.ds(CO, 2), inner_x, inner_y, :],
            dst_ref=field.at[pl.ds(CO, 2), to_x, to_y, :],
            send_sem=halo_send.at[slot],
            recv_sem=halo_recv.at[slot],
            device_id={"gx": gx + dx, "gy": gy + dy},
            device_id_type=MESH,
        )

    order = [(0, 1), (0, -1), (1, 0), (-1, 0), (1, -1), (-1, 1), (1, 1), (-1, -1)]
    aux_order = [side for side in order if side not in ((1, 1), (-1, -1))]

    for dx, dy in order:

        @pl.when(inside(dx, dy))
        def _(dx=dx, dy=dy):
            for copy in halo(dx, dy):
                copy.start()

    def start_aux():
        for dx, dy in aux_order:

            @pl.when(inside(dx, dy))
            def _(dx=dx, dy=dy):
                aux(dx, dy).start()

    @pl.when(gx == 0)
    def _():
        field[:, 0:2] = jnp.zeros((8, 2, ROWS, 128), F32)

    @pl.when(gx == n_x - 1)
    def _():
        field[:, 18:20] = jnp.zeros((8, 2, ROWS, 128), F32)

    @pl.when(gy == 0)
    def _():
        field[:, 0:20, 0:2, :] = jnp.zeros((8, 20, 2, 128), F32)

    @pl.when(gy == n_y - 1)
    def _():
        field[:, 0:20, 18:20, :] = jnp.zeros((8, 20, 2, 128), F32)

    eye = lax.broadcasted_iota(jnp.int32, (16, 16), 0) == lax.broadcasted_iota(
        jnp.int32, (16, 16), 1
    )
    loads[7].wait()
    lane16 = lax.broadcasted_iota(jnp.int32, (16, 128), 1)
    on_plane = lane16 == plane_ref[0]

    def make_drive(x):
        line = jnp.broadcast_to(amp_ref[0, pl.ds(x, 1), :], (16, 16))
        column = jnp.sum(jnp.where(eye, line, 0.0), axis=1, keepdims=True)
        field[DR, x + 2, pl.ds(2, 16), :] = jnp.where(
            on_plane, jnp.broadcast_to(column, (16, 128)), 0.0
        )

    loop(0, 16, 4, make_drive)

    loads[2].wait()

    def make_coef(p):
        field[CO, p, pl.ds(2, 16), :] = courant / field[CO, p, pl.ds(2, 16), :]

    loop(2, 16, 4, make_coef)

    start_aux()

    total_x = n_x * 16
    total_y = n_y * 16

    def profile(cells, total, width):
        place = cells.astype(F32)
        dist = jnp.minimum(place, total - 1.0 - place)
        wide = jnp.full(cells.shape, width, jnp.int32).astype(F32)
        return jnp.maximum(0.0, (wide - dist) / wide) ** 2

    loads[5].wait()
    ys = gy * 16 - 2 + lax.broadcasted_iota(jnp.int32, (ROWS, 128), 0)
    prof_y = profile(ys, total_y, pml_ref[1])
    in_y = (ys >= 0) & (ys < total_y)

    def make_damp(p):
        xs = jnp.full((ROWS, 128), gx * 16 - 2 + p, jnp.int32)
        value = jnp.exp(-absorb * (profile(xs, total_x, pml_ref[0]) + prof_y))
        keep = in_y & (xs >= 0) & (xs < total_x)
        damp[p] = jnp.where(keep, value, 0.0)

    loop(0, 20, 4, make_damp)

    pl.semaphore_wait(round1, 4)
    for x in (2, 1, 3):
        tell(round2, x=x)
    tell(round2, c=1)

    loads[6].wait()
    row_id = lax.broadcasted_iota(jnp.int32, (8, 128), 0)
    tval = (row_id % 2 + 1).astype(F32)
    omega = jnp.where(
        row_id < 2, jnp.full((8, 128), freq_ref[0, 0]), jnp.full((8, 128), freq_ref[0, 1])
    )
    trig[0:8] = jnp.cos(omega * tval)
    trig[8:16] = jnp.sin(omega * tval)

    loads[8].wait()
    loads[3].wait()
    loads[4].wait()

    blocks = blocks_ref[...]
    masks = []
    for bx in range(2):
        for by in range(2):
            cell = (gx * 2 + bx) * (total_y // BS) + gy * 2 + by
            hit = jnp.where(blocks == cell, 1.0, 0.0)
            masks.append(jnp.max(hit, axis=1, keepdims=True))
    upper = lax.broadcasted_iota(jnp.int32, (16, 128), 0) < 8

    def make_weights(bx):
        mask = jnp.where(
            upper,
            jnp.broadcast_to(masks[2 * bx], (16, 128)),
            jnp.broadcast_to(masks[2 * bx + 1], (16, 128)),
        )

        def step(x):
            for k in range(2):
                c1 = trig[pl.ds(2 * k, 1), :]
                c2 = trig[pl.ds(2 * k + 1, 1), :]
                s1 = trig[pl.ds(8 + 2 * k, 1), :]
                s2 = trig[pl.ds(8 + 2 * k + 1, 1), :]
                first = None
                for c in range(3):
                    fr = fwd[k, 0, c, x].astype(F32) * mask
                    fi = fwd[k, 1, c, x].astype(F32) * mask
                    ar = adj[k, 0, c, x].astype(F32)
                    ai = adj[k, 1, c, x].astype(F32)
                    part = fr * ar + fi * ai
                    first = part if first is None else first + part
                    weights[x, k * 7 + 1 + c, pl.ds(2, 16), :] = fr * c1 - fi * s1
                    weights[x, k * 7 + 4 + c, pl.ds(2, 16), :] = fr * c2 - fi * s2
                weights[x, k * 7, pl.ds(2, 16), :] = first

        loop(bx * 8, 8, 1, step)

    make_weights(0)
    make_weights(1)

    loads[0].wait()
    loads[1].wait()

    for dx, dy in order:

        @pl.when(inside(-dx, -dy))
        def _(dx=dx, dy=dy):
            for copy in halo(dx, dy):
                copy.wait_recv()
            if (dx, dy) in aux_order:
                aux(dx, dy).wait_recv()

    lane = lax.broadcasted_iota(jnp.int32, (ROWS, 128), 1)
    not_last = lane < 127
    not_first = lane > 0

    def ahead_z(v):
        return jnp.where(not_last, pltpu.roll(v, 127, 1), 0.0) - v

    def behind_z(v):
        return v - jnp.where(not_first, pltpu.roll(v, 1, 1), 0.0)

    def ahead_y(v):
        return pltpu.roll(v, ROWS - 1, 0) - v

    def behind_y(v):
        return v - pltpu.roll(v, 1, 0)

    def magnetic(p, e, ahead, h):
        d = damp[p]
        ex, ey, ez = e
        hx = d * (h[0] - courant * (ahead_y(ez) - ahead_z(ey)))
        hy = d * (h[1] - courant * (ahead_z(ex) - (ahead[2] - ez)))
        hz = d * (h[2] - courant * ((ahead[1] - ey) - ahead_y(ex)))
        return hx, hy, hz

    def electric(p, h, behind, e, sine):
        d = damp[p]
        co = field[CO, p]
        hx, hy, hz = h
        ex = d * (e[0] + co * (behind_y(hz) - behind_z(hy)))
        ey = d * (e[1] + co * (behind_z(hx) - (hz - behind[2])))
        ez = d * (e[2] + co * ((hy - behind[1]) - behind_y(hx)) + field[DR, p] * sine)
        return ex, ey, ez

    sine1 = trig[pl.ds(8, 1), :]
    sine2 = trig[pl.ds(9, 1), :]

    def read(first, p):
        return tuple(field[first + c, p] for c in range(3))

    others = [(1, 2), (1, 1), (1, 3), (1, 0), (0, 2), (0, 1), (0, 3)]

    def peer(dz, dx):
        return (z_hi + dz) % 2, (lane_x + dx) % 4

    def send_planes(first, count):
        for dz, dx in others:
            k, j = peer(dz, dx)
            pltpu.make_async_remote_copy(
                src_ref=term.at[k, j, pl.ds(first, count), pl.ds(2, 16), :],
                dst_ref=landed.at[grp, pl.ds(first, count)],
                send_sem=red_send,
                recv_sem=red_recv,
                device_id={"grp": k * 4 + j},
                device_id_type=MESH,
            ).start()

    e0 = read(EX, 0)
    h1 = e1 = h2 = None
    for p in range(19):
        e0_next = read(EX, p + 1)
        h1_last, e1_last, h2_last = h1, e1, h2
        h1 = magnetic(p, e0, e0_next, read(HX, p))
        if p >= 1:
            e1 = electric(p, h1, h1_last, e0, sine1)
        if p >= 2:
            h2 = magnetic(p - 1, e1_last, e1, h1_last)
        if p >= 3:
            e2 = electric(p - 1, h2, h2_last, e1_last, sine2)
            x = p - 3
            for k in range(2):
                value = weights[x, k * 7]
                for c in range(3):
                    value = value + weights[x, k * 7 + 1 + c] * e1_last[c]
                    value = value + weights[x, k * 7 + 4 + c] * e2[c]
                term[k, x % 4, x // 4] = value
            if x == READY[0]:
                pl.semaphore_wait(round2, 4)
            if x in READY:
                first = 0 if x == READY[0] else 1 + READY[READY.index(x) - 1] // 4
                send_planes(first, x // 4 + 1 - first)
        e0 = e0_next

    landed[grp] = term[z_hi, lane_x, :, 2:18, :]
    seven = landed.at[pl.ds(0, 7)]
    pltpu.make_async_copy(seven, seven, red_recv).wait()

    total = landed[0]
    for j in range(1, 8):
        total = total + landed[j]
    summed[...] = total
    square = jnp.sum(total * total, axis=0)
    line = jnp.sum(square, axis=0, keepdims=True)

    me1 = place * 2 + core
    me2 = gy * 4 + lane_x
    row1[...] = line
    rows1[pl.ds(me1, 1), :] = line
    steps = [(dz, dc) for dz in range(8) for dc in range(2) if (dz, dc) != (0, 0)]
    for dz, dc in sorted(steps, key=lambda d: -min(d[0], 8 - d[0])):
        pltpu.make_async_remote_copy(
            src_ref=row1,
            dst_ref=rows1.at[pl.ds(me1, 1)],
            send_sem=s1_send,
            recv_sem=s1_recv,
            device_id=device(z=dz, c=dc),
            device_id_type=MESH,
        ).start()

    mine = grad_out.at[z_hi, :, lane_x]
    out = pltpu.make_async_copy(summed, mine, out_sem)
    out.start()
    for dz, dx in others:
        k, j = peer(dz, dx)
        pltpu.make_async_remote_copy(
            src_ref=summed,
            dst_ref=mine,
            send_sem=gat_send,
            recv_sem=gat_recv,
            device_id={"grp": k * 4 + j},
            device_id_type=MESH,
        ).start()

    some = rows1.at[pl.ds(0, 15)]
    pltpu.make_async_copy(some, some, s1_recv).wait()
    for k in range(2):
        line = jnp.sum(rows1[8 * k : 8 * k + 8], axis=0, keepdims=True)
        row2[k] = line
        rows2[k, pl.ds(me2, 1), :] = line
    steps = [(dy, dx) for dy in range(8) for dx in range(4) if (dy, dx) != (0, 0)]
    for dy, dx in sorted(steps, key=lambda d: -min(d[0], 8 - d[0]) - min(d[1], 4 - d[1])):
        pltpu.make_async_remote_copy(
            src_ref=row2,
            dst_ref=rows2.at[:, pl.ds(me2, 1)],
            send_sem=s2_send,
            recv_sem=s2_recv,
            device_id=device(y=dy, x=dx),
            device_id_type=MESH,
        ).start()

    for dx, dy in order:

        @pl.when(inside(dx, dy))
        def _(dx=dx, dy=dy):
            for copy in halo(dx, dy):
                copy.wait_send()
            if (dx, dy) in aux_order:
                aux(dx, dy).wait_send()

    pltpu.make_async_copy(seven, seven, red_send).wait()
    pltpu.make_async_copy(seven, seven, gat_send).wait()
    pltpu.make_async_copy(some, some, s1_send).wait()
    out.wait()
    pltpu.make_async_copy(seven, seven, gat_recv).wait()

    few = rows2.at[:, pl.ds(0, 31)]
    pltpu.make_async_copy(few, few, s2_recv).wait()
    count = float(128 * BS * BS * 128)
    for k in range(2):
        squares = jnp.sum(rows2[k], axis=0, keepdims=True)
        squares = jnp.sum(squares, axis=1, keepdims=True)
        value = lax.rsqrt(squares / count + 1e-05)
        scale_ref[k] = jnp.broadcast_to(value, (8, 128))
    pltpu.make_async_copy(few, few, s2_send).wait()


def body(
    efield,
    hfield,
    fwd_dft,
    adj_dft,
    permittivity,
    source_amp,
    source_plane,
    freqs,
    pml_width,
    design_blocks,
):
    hbm = pl.BlockSpec(memory_space=pltpu.HBM)
    def pin(value):
        return pltpu.with_memory_space_constraint(value, pltpu.HBM)

    vmem = pl.BlockSpec(memory_space=pltpu.VMEM)
    dma = pltpu.SemaphoreType.DMA
    grad, scale = pl.pallas_call(
        kernel,
        out_shape=(
            jax.ShapeDtypeStruct((2, 4, 4, 16, 128), F32),
            jax.ShapeDtypeStruct((2, 8, 128), F32),
        ),
        in_specs=[hbm] * 6 + [pl.BlockSpec(memory_space=pltpu.SMEM)] + [hbm] * 3,
        out_specs=(pl.BlockSpec(memory_space=pl.ANY), vmem),
        scratch_shapes=[
            pltpu.VMEM((8, PLANES, ROWS, 128), F32),
            pltpu.VMEM((20, ROWS, 128), F32),
            pltpu.VMEM((2, 2, 3, 16, 16, 128), jnp.bfloat16),
            pltpu.VMEM((2, 2, 3, 16, 16, 128), jnp.bfloat16),
            pltpu.VMEM((16, 128), F32),
            pltpu.VMEM((16, 14, ROWS, 128), F32),
            pltpu.VMEM((2, 4, 4, ROWS, 128), F32),
            pltpu.VMEM((8, 4, 16, 128), F32),
            pltpu.VMEM((4, 16, 128), F32),
            pltpu.VMEM((1, 128), F32),
            pltpu.VMEM((16, 128), F32),
            pltpu.VMEM((2, 1, 128), F32),
            pltpu.VMEM((2, 32, 128), F32),
            pltpu.VMEM((1, 16, 16), F32),
            pltpu.SMEM((1, 2), F32),
            pltpu.SMEM((2,), jnp.int32),
            pltpu.VMEM((1, 128), jnp.int32),
            dma((9,)),
            dma((32,)),
            dma((32,)),
            dma,
            dma,
            dma,
            dma,
            dma,
            dma,
            dma,
            dma,
            dma,
            pltpu.SemaphoreType.REGULAR,
            pltpu.SemaphoreType.REGULAR,
        ],
        compiler_params=pltpu.CompilerParams(
            collective_id=0, has_side_effects=True, vmem_limit_bytes=40 * 1024 * 1024
        ),
        name="adjoint",
    )(
        *map(pin, (efield, hfield, fwd_dft, adj_dft, permittivity, source_amp)),
        source_plane,
        *map(pin, (freqs, pml_width, design_blocks[None, :])),
    )
    return grad.reshape(2, 16, 16, 128) * scale[:, :1, None, :]


def solution(mesh):
    in_specs = (
        P("grp", None, "gx", "gy", None),
        P("grp", None, "gx", "gy", None),
        P("grp", None, None, None, "gx", "gy", None),
        P("grp", None, None, None, "gx", "gy", None),
        P("gx", "gy", None),
        P("grp", "gx", "gy"),
        P("grp"),
        P("grp", None),
        P(),
        P(),
    )
    out_specs = P(None, "gx", "gy", None)
    return jax.shard_map(body, mesh=mesh, in_specs=in_specs, out_specs=out_specs, check_vma=False)
```
